32 devices in a mesh: groups: 2 (over y), dom: 4 (over z), chan: 2 (over x), rep: 2 (over core).
Axes of the slice: x: 2, y: 2, z: 4, core: 2. Of those that a mesh axis runs over, the one named last changes fastest.
Arguments:
- node_feats: bfloat16 [4096, 1024], P(('groups', 'dom', 'rep'), 'chan'), parts along dimension 0, may hold values from -6 to 6
- edge_feats: bfloat16 [24576, 1024], P(('groups', 'dom', 'rep'), 'chan'), parts along dimension 0, may hold values from -6 to 6
- senders: int32 [24576], P(('groups', 'dom', 'rep')), parts along dimension 0, may hold values from 0 to 255
- receiver_slot: int32 [24576], P(('groups', 'dom', 'rep')), parts along dimension 0, may hold values from 0 to 511
- halo_rows: int32 [16, 4, 64], P(('groups', 'dom', 'rep')), parts along dimension 0, may hold values from 0 to 255
- tile_counts: int32 [16], P('groups'), parts along dimension 0, may hold values from 1 to 12, as said below
- weight_in: bfloat16 [3, 1024, 1024], P(None, 'chan'), may hold values from -0.109375 to 0.109375
- weight_out: bfloat16 [1024, 1024], P(None, 'chan'), may hold values from -0.1875 to 0.1875
- norm_gain: float32 [1024], P('chan'), may hold values from 0.25 to 1.75
Outputs:
- updated_edges: bfloat16 [24576, 1024], P(('groups', 'dom', 'rep'), 'chan'), parts along dimension 0
- aggregated: float32 [4096, 1024], P(('groups', 'dom', 'rep'), 'chan'), parts along dimension 0
The draws below stay inside these ranges and needn't reach their ends.
There are 2 independent parts, one for each index of `groups`. The reference program is written for one: setup_inputs(seed, part) draws one part's arguments, and reference() takes and returns one part's arrays. A program takes and returns all parts, laid end to end along the dimension named above; an argument that names none is the same for every part. Nothing has to cross between parts.
Inputs may be any that keep to these rules, and one draw needn't show every extreme that they name: `tile_counts`: A partition with more than 9 live tiles has all 12; then the partition 8 / 2 further on the cycle holds at most 6 and no other partition holds more than 9.
All inputs are finite; a program needn't handle non-finite values.
Results may differ from the reference program's by a relative error of at most 0.0033.
Values may be sent and summed in bfloat16 or wider, within the bound.
No kernel may reach another device: no remote copies, remote signals or barrier semaphores. Data moves between devices by JAX's collectives and lax.ppermute only.
A program may use at most 64 MiB of HBM per device.

```python
import jax
import jax.numpy as jnp
from jax import lax

C = 1024
NP = 256
TILE = 128
TILES = 12
WORK = 9
SHIP = 3
RADIUS = 2
HALO = 64
PARTS_SIZE = 8
NODES = 2048
ECAP = 1536
EDGES = 12288


def draw_tile_counts(key, part):
    key = jax.random.fold_in(key, 11)
    first_key, second_key, third_key = jax.random.split(key, 3)
    region_start = jax.random.randint(first_key, (), 0, PARTS_SIZE)
    cycle_offset = (jnp.arange(PARTS_SIZE) - region_start) % PARTS_SIZE
    overloaded = cycle_offset < PARTS_SIZE // 4
    partners = (cycle_offset >= PARTS_SIZE // 2) & (cycle_offset < PARTS_SIZE // 2 + PARTS_SIZE // 4)
    light_counts = jax.random.randint(second_key, (PARTS_SIZE,), 1, WORK - SHIP + 1)
    light_counts = jnp.where(cycle_offset == PARTS_SIZE // 2, WORK - SHIP, light_counts)
    other_counts = jax.random.randint(third_key, (PARTS_SIZE,), 1, WORK + 1)
    other_counts = jnp.where(cycle_offset == PARTS_SIZE // 4, WORK, other_counts)
    counts = jnp.where(overloaded, TILES, jnp.where(partners, light_counts, other_counts))
    return counts.astype(jnp.int32)


def with_ends(values, own_key, smallest, largest):
    spot = [jax.random.randint(jax.random.fold_in(own_key, axis), (), 0, length) for axis, length in enumerate(values.shape)]
    widest = values.shape.index(max(values.shape))
    next_to = spot[:widest] + [(spot[widest] + 1) % values.shape[widest]] + spot[widest + 1:]
    return values.at[tuple(spot)].set(smallest).at[tuple(next_to)].set(largest)


def steps_of(rng, extent, shards, least, top_value):
    loudness, own = 1.0, jax.random.fold_in(rng, 6)
    for dim, blocks in shards:
        heights = jnp.exp(jax.random.uniform(jax.random.fold_in(own, dim), (blocks,), jnp.float32, least / len(shards), top_value / len(shards)))
        loudness = loudness * jnp.repeat(heights, extent[dim] // blocks).reshape([-1 if axis == dim else 1 for axis in range(len(extent))])
    return loudness


def bell_draw(rng, shape, width, bound, cuts=(), kind=jnp.bfloat16):
    level = steps_of(rng, shape, cuts, -0.22, 0.18) if cuts else 1.0
    values = jax.random.normal(rng, shape, jnp.float32) * width * level
    return jnp.minimum(jnp.maximum(values, -bound), bound).astype(kind)


def setup_inputs(seed: int = 0, part: int = 0) -> dict:
    splits = jax.random.split(jax.random.key(seed), 10)
    part_splits = jax.random.split(jax.random.fold_in(splits[9], part), 10)
    node_feats = bell_draw(part_splits[0], (NODES, C), 1.0, 6.0, ((0, 8), (1, 2)))
    edge_feats = bell_draw(part_splits[1], (EDGES, C), 1.0, 6.0, ((0, 8), (1, 2)))
    senders = with_ends(jax.random.randint(part_splits[2], (EDGES,), 0, NP), jax.random.fold_in(part_splits[2], 1), 0, NP - 1).astype(jnp.int32)
    receiver_slot = with_ends(jax.random.randint(part_splits[3], (EDGES,), 0, NP + 2 * RADIUS * HALO), jax.random.fold_in(part_splits[3], 1), 0, (NP + 2 * RADIUS * HALO) - 1).astype(jnp.int32)
    halo_rows = with_ends(jax.random.randint(part_splits[4], (PARTS_SIZE, 2 * RADIUS, HALO), 0, NP), jax.random.fold_in(part_splits[4], 1), 0, NP - 1).astype(jnp.int32)
    tile_counts = draw_tile_counts(jax.random.fold_in(jax.random.fold_in(splits[9], part), 71), part)
    weight_in = bell_draw(splits[6], (3, C, C), (3 * C) ** -0.5, 0.109375, ((1, 2),))
    weight_out = bell_draw(splits[7], (C, C), C ** -0.5, 0.1875, ((1, 2),))
    norm_gain = jnp.clip(1.0 + 0.15 * jax.random.normal(splits[8], (C,), jnp.float32), 0.25, 1.75)
    return {"node_feats": node_feats, "edge_feats": edge_feats, "senders": senders, "receiver_slot": receiver_slot, "halo_rows": halo_rows, "tile_counts": tile_counts, "weight_in": weight_in, "weight_out": weight_out, "norm_gain": norm_gain}


def reference(node_feats, edge_feats, senders, receiver_slot, halo_rows, tile_counts, weight_in, weight_out, norm_gain):
    offsets = [shift_by for shift_by in range(-RADIUS, RADIUS + 1) if shift_by != 0]

    def partition_update(part_index):
        edge_block = lax.dynamic_slice_in_dim(edge_feats, part_index * ECAP, ECAP, 0)
        sender_ids = lax.dynamic_slice_in_dim(senders, part_index * ECAP, ECAP, 0) + part_index * NP
        slots = lax.dynamic_slice_in_dim(receiver_slot, part_index * ECAP, ECAP, 0)
        id_tables = [part_index * NP + jnp.arange(NP, dtype=jnp.int32)]
        for slot_index, shift_by in enumerate(offsets):
            source = ((part_index - shift_by) % PARTS_SIZE).astype(jnp.int32)
            rows_sent = lax.dynamic_index_in_dim(halo_rows, source, 0, keepdims=False)[slot_index]
            id_tables.append(source * NP + rows_sent)
        receivers = jnp.concatenate(id_tables)[slots]
        preact = jnp.dot(edge_block, weight_in[0], preferred_element_type=jnp.float32)
        preact = preact + jnp.dot(node_feats[sender_ids], weight_in[1], preferred_element_type=jnp.float32)
        preact = preact + jnp.dot(node_feats[receivers], weight_in[2], preferred_element_type=jnp.float32)
        hidden = jax.nn.silu(preact).astype(jnp.bfloat16)
        projected = jnp.dot(hidden, weight_out, preferred_element_type=jnp.float32)
        row_mean = lax.optimization_barrier(jnp.mean(projected, axis=1))
        row_var = lax.optimization_barrier(jnp.mean(projected * projected, axis=1)) - row_mean * row_mean
        normed = (projected - row_mean[:, None]) * lax.rsqrt(row_var + 1e-05)[:, None] * norm_gain
        updated = (edge_block.astype(jnp.float32) + normed).astype(jnp.bfloat16)
        live_mask = jnp.arange(ECAP, dtype=jnp.int32) < TILE * tile_counts[part_index]
        finished = jnp.where(live_mask[:, None], updated, edge_block)
        return (finished, receivers, live_mask)
    finished, receivers, live_mask = lax.map(partition_update, jnp.arange(PARTS_SIZE, dtype=jnp.int32))
    updated_edges = finished.reshape(EDGES, C)
    messages = jnp.where(live_mask.reshape(EDGES)[:, None], updated_edges.astype(jnp.float32), jnp.float32(0.0))
    aggregated = jax.ops.segment_sum(messages, receivers.reshape(EDGES), num_segments=NODES)
    return (updated_edges, aggregated)
```

```python
import jax
import jax.numpy as jnp
from jax import lax
from jax.sharding import PartitionSpec as P

TILE = 128
RADIUS = 2
CHUNKS = 3
bf16 = jnp.bfloat16
f32 = jnp.float32


def shifted(block, axis, distance):
    size = lax.axis_size(axis)
    return lax.ppermute(block, axis, [(i, (i + distance) % size) for i in range(size)])


def swapped(block, axis):
    size = lax.axis_size(axis)
    return lax.ppermute(block, axis, [(i, i ^ 1) for i in range(size)])


def fetch(block, dim, distance, order):
    share = sum((lax.axis_index(axis) % 2) << place for place, axis in enumerate(order))
    rows = block.shape[dim] >> len(order)
    piece = lax.dynamic_slice_in_dim(block, share * rows, rows, dim)
    piece = shifted(piece, "chan", distance)
    for axis in order:
        other = swapped(piece, axis)
        first = lax.axis_index(axis) % 2 == 0
        piece = jnp.where(
            first,
            jnp.concatenate([piece, other], axis=dim),
            jnp.concatenate([other, piece], axis=dim),
        )
    return piece


def onehot(rows, columns, live=None):
    hit = rows[:, None] == columns[None, :]
    if live is not None:
        hit = hit & live
    return hit.astype(bf16)


def local(
    node_feats,
    edge_feats,
    senders,
    receiver_slot,
    halo_rows,
    tile_counts,
    weight_in,
    weight_out,
    norm_gain,
):
    ways = lax.axis_size("chan")
    me = lax.axis_index("chan")
    my_index = lax.axis_index(("dom", "rep"))
    offsets = [shift_by for shift_by in range(-RADIUS, RADIUS + 1) if shift_by != 0]
    local_nodes, width = node_feats.shape
    halo_size = halo_rows.shape[2]
    slot_count = edge_feats.shape[0]
    channels = ways * width
    table_rows = local_nodes + len(offsets) * halo_size
    chunk = slot_count // CHUNKS
    mine = chunk // ways
    pairs = [axis for axis in ("groups", "dom", "rep") if lax.axis_size(axis) % 2 == 0]
    order = pairs
    other_order = [axis for axis in ("dom", "groups", "rep") if axis in pairs]
    distances = range(1, ways)

    nodes = [node_feats] + [shifted(node_feats, "chan", d) for d in distances]
    gains = [norm_gain] + [shifted(norm_gain, "chan", d) for d in distances]
    first_pair = [weight_in[:2]] + [fetch(weight_in[:2], 1, d, order) for d in distances]
    third = [weight_in[2]] + [fetch(weight_in[2], 0, d, other_order) for d in distances]
    outs = [weight_out] + [fetch(weight_out, 0, d, other_order) for d in distances]

    def rows_of(array, k, owner):
        return lax.dynamic_slice_in_dim(array, k * chunk + owner * mine, mine, 0)

    edges = [
        [rows_of(edge_feats, k, me)]
        + [shifted(rows_of(edge_feats, k, (me + d) % ways), "chan", d) for d in distances]
        for k in range(CHUNKS)
    ]

    full_nodes = jnp.concatenate(nodes, axis=1)
    node_ids = jnp.arange(local_nodes, dtype=jnp.int32)
    incoming = []
    for j, shift_by in enumerate(offsets):
        rows = jnp.dot(onehot(halo_rows[0, j], node_ids), full_nodes, preferred_element_type=f32)
        incoming.append(shifted(rows.astype(bf16), ("dom", "rep"), shift_by))
    extended = jnp.concatenate([full_nodes] + incoming, axis=0)

    slot_ids = jnp.arange(table_rows, dtype=jnp.int32)
    whole_in = jnp.concatenate(
        [w[0] for w in first_pair] + [w[1] for w in first_pair] + third, axis=0
    )
    whole_out = jnp.concatenate(outs, axis=1)
    gain = jnp.concatenate(gains)
    live_rows = TILE * tile_counts[my_index]

    slot_sums = jnp.zeros((table_rows, width), f32)
    finished = []
    for k in range(CHUNKS):
        sender = rows_of(senders, k, me)
        slot = rows_of(receiver_slot, k, me)
        own = jnp.concatenate(edges[k], axis=1)
        sent = jnp.dot(onehot(sender, node_ids), full_nodes, preferred_element_type=f32)
        got = jnp.dot(onehot(slot, slot_ids), extended, preferred_element_type=f32)
        joined = jnp.concatenate([own, sent.astype(bf16), got.astype(bf16)], axis=1)
        preact = jnp.dot(joined, whole_in, preferred_element_type=f32)
        hidden = jax.nn.silu(preact).astype(bf16)
        projected = jnp.dot(hidden, whole_out, preferred_element_type=f32)
        row_mean = jnp.sum(projected, axis=1, keepdims=True) / channels
        row_square = jnp.sum(projected * projected, axis=1, keepdims=True) / channels
        scale = lax.rsqrt(row_square - row_mean * row_mean + 1e-05)
        normed = (projected - row_mean) * scale * gain
        edge_ids = k * chunk + me * mine + jnp.arange(mine, dtype=jnp.int32)
        live = (edge_ids < live_rows)[:, None]
        updated = jnp.where(live, (own.astype(f32) + normed).astype(bf16), own)
        parts = [updated[:, d * width : (d + 1) * width] for d in range(ways)]
        parts = [parts[0]] + [shifted(parts[d], "chan", -d) for d in distances]
        whole = jnp.zeros((chunk, width), bf16)
        for d in range(ways):
            whole = lax.dynamic_update_slice_in_dim(whole, parts[d], ((me + d) % ways) * mine, 0)
        finished.append(whole)
        slots = receiver_slot[k * chunk : (k + 1) * chunk]
        chunk_live = (k * chunk + jnp.arange(chunk, dtype=jnp.int32)) < live_rows
        slot_sums += jnp.dot(
            onehot(slot_ids, slots, chunk_live[None, :]), whole, preferred_element_type=f32
        )
    own_sums = slot_sums[:local_nodes]
    returned = []
    for j, shift_by in enumerate(offsets):
        start = local_nodes + j * halo_size
        piece = slot_sums[start : start + halo_size].astype(bf16)
        returned.append(shifted(piece, ("dom", "rep"), -shift_by))
    aggregated = own_sums + jnp.dot(
        onehot(node_ids, halo_rows[0].reshape(-1)),
        jnp.concatenate(returned, axis=0),
        preferred_element_type=f32,
    )
    return (jnp.concatenate(finished, axis=0), aggregated)


def solution(mesh):
    placed = (
        P(("groups", "dom", "rep"), "chan"),
        P(("groups", "dom", "rep"), "chan"),
        P(("groups", "dom", "rep")),
        P(("groups", "dom", "rep")),
        P(("groups", "dom", "rep"), None, None),
        P("groups"),
        P(None, "chan", None),
        P(None, "chan"),
        P("chan"),
    )
    return jax.shard_map(
        local,
        mesh=mesh,
        in_specs=placed,
        out_specs=(P(("groups", "dom", "rep"), "chan"), P(("groups", "dom", "rep"), "chan")),
        check_vma=False,
    )
```

```python
import functools

import jax
import jax.numpy as jnp
from jax import lax
from jax.experimental import pallas as pl
from jax.experimental.pallas import tpu as pltpu
from jax.sharding import PartitionSpec as P

TILE = 128
RADIUS = 2
GAIN_ROWS = 16
SHARERS_A = ("dom", "rep")
SHARERS_B = ("groups", "rep")
bf16 = jnp.bfloat16
f32 = jnp.float32
i32 = jnp.int32
VMEM_BYTES = 24 * 1024 * 1024
PREPARE_VMEM_BYTES = 60 * 1024 * 1024
HBM = pl.BlockSpec(memory_space=pltpu.HBM)
VMEM = pl.BlockSpec(memory_space=pltpu.VMEM)
SMEM = pl.BlockSpec(memory_space=pltpu.SMEM)


def shape(*dims, dtype=bf16):
    return jax.ShapeDtypeStruct(dims, dtype)


def params(vmem=VMEM_BYTES):
    return pltpu.CompilerParams(vmem_limit_bytes=vmem)


def shifted(block, axis, distance):
    size = lax.axis_size(axis)
    return lax.ppermute(block, axis, [(i, (i + distance) % size) for i in range(size)])


def swapped(block, axis):
    size = lax.axis_size(axis)
    return lax.ppermute(block, axis, [(i, i ^ 1) for i in range(size)])


def even(axes):
    return [axis for axis in axes if lax.axis_size(axis) % 2 == 0]


def share_index(axes):
    return sum((lax.axis_index(axis) % 2) << place for place, axis in enumerate(axes))


def tie(array, *others):
    return lax.optimization_barrier((array, *others))[0]


def dot(a, b):
    return jnp.dot(a, b, preferred_element_type=f32)


def column(row):
    return jnp.transpose(jnp.broadcast_to(row, (128, row.shape[1])))


def onehot(ids, count):
    lanes = lax.broadcasted_iota(i32, ids.shape, 1)
    hits = [(ids == lanes + base).astype(f32).astype(bf16) for base in range(0, count, 128)]
    return jnp.concatenate(hits, axis=1) if len(hits) > 1 else hits[0]


def copier(sems):
    copies = []

    def copy(source, target):
        copies.append(pltpu.make_async_copy(source, target, sems.at[len(copies)]))
        copies[-1].start()

    def finish():
        for c in copies:
            c.wait()

    return copy, finish


def share_kernel(ways, axes_a, axes_b, w_in, w_out, nodes, gain, first, second, sems):
    copy, finish = copier(sems)
    width = w_out.shape[1]
    rows_a, rows_b = width >> len(axes_a), width >> len(axes_b)
    start_a = pl.multiple_of(share_index(axes_a) * rows_a, rows_a)
    start_b = pl.multiple_of(share_index(axes_b) * rows_b, rows_b)
    for part in range(2):
        copy(w_in.at[part, pl.ds(start_a, rows_a), :], first.at[pl.ds(part * rows_a, rows_a), :])
    copy(w_in.at[2, pl.ds(start_b, rows_b), :], second.at[0])
    for h in range(ways):
        copy(w_out.at[pl.ds(h * width + start_b, rows_b), :], second.at[1, :, pl.ds(h * width, width)])
    base = 2 * rows_a
    count = nodes.shape[0] // ways
    for h in range(ways):
        copy(nodes.at[pl.ds(h * count, count), :], first.at[pl.ds(base, count), pl.ds(h * width, width)])
    high = gain[...].astype(bf16)
    middle = (gain[...] - high.astype(f32)).astype(bf16)
    low = (gain[...] - high.astype(f32) - middle.astype(f32)).astype(bf16)
    row_ids = lax.broadcasted_iota(i32, (GAIN_ROWS, width), 0)
    rows = jnp.where(row_ids == 0, high.astype(f32), 0.0)
    rows = jnp.where(row_ids == 1, middle.astype(f32), rows)
    rows = jnp.where(row_ids == 2, low.astype(f32), rows)
    first[base + count :, :] = jnp.concatenate([rows.astype(bf16)] * ways, axis=1)
    finish()


def prepare_shares(weight_in, weight_out, nodes, gain, ways, axes_a, axes_b):
    width = weight_out.shape[1]
    rows = 2 * (width >> len(axes_a)) + nodes.shape[0] // ways + GAIN_ROWS
    return pl.pallas_call(
        functools.partial(share_kernel, ways, axes_a, axes_b),
        out_shape=[shape(rows, ways * width), shape(2, width >> len(axes_b), ways * width)],
        in_specs=[HBM, HBM, HBM, VMEM],
        out_specs=[VMEM] * 2,
        scratch_shapes=[pltpu.SemaphoreType.DMA((3 + 2 * ways,))],
        compiler_params=params(PREPARE_VMEM_BYTES),
        name="prepare_shares",
    )(weight_in, weight_out, nodes, gain)


def block_kernel(ways, edges, *rest):
    blocks, sems = rest[:-1], rest[-1]
    copy, finish = copier(sems)
    me = lax.axis_index("chan")
    mine = edges.shape[0] // ways
    for d in range(1, ways):
        row = pl.multiple_of(lax.rem(me + d, ways) * mine, TILE)
        copy(edges.at[pl.ds(row, mine), :], blocks[d - 1])
    finish()


def prepare_blocks(edge_feats, ways):
    slot_count, width = edge_feats.shape
    return pl.pallas_call(
        functools.partial(block_kernel, ways),
        out_shape=[shape(slot_count // ways, width)] * (ways - 1),
        in_specs=[HBM],
        out_specs=[VMEM] * (ways - 1),
        scratch_shapes=[pltpu.SemaphoreType.DMA((ways - 1,))],
        compiler_params=params(),
        name="prepare_blocks",
    )(edge_feats)


def unpack_kernel(ways, halo_count, rows_ref, nodes, *refs):
    messages, outs = refs[: ways - 1], list(refs[ways - 1 :])
    halos = [outs.pop(0) for _ in range(halo_count)]
    pieces, others, gains = (outs[i :: 3] for i in range(3))
    count, width = nodes.shape
    for d in range(1, ways):
        message, piece, other, gain = messages[d - 1], pieces[d - 1], others[d - 1], gains[d - 1]
        rows = piece.shape[1]
        for part in range(2):
            piece[part] = message[part * rows : (part + 1) * rows, :]
        base, packed = 2 * rows, count // ways
        for h in range(ways):
            other[h * packed : (h + 1) * packed, :] = message[base : base + packed, h * width : (h + 1) * width]
        parts = message[base + packed :, :width].astype(f32)
        gain[...] = parts[0:1, :] + parts[1:2, :] + parts[2:3, :]
    for j in range(halo_count):
        hits = onehot(column(rows_ref[0, j : j + 1, :]), count)
        for d in range(ways):
            table = nodes[...] if d == 0 else others[d - 1][...]
            halos[j][:, d * width : (d + 1) * width] = dot(hits, table).astype(bf16)


def unpack(halo_rows, nodes, messages, ways, axes_a):
    _, offsets, size = halo_rows.shape
    count, width = nodes.shape
    each = [shape(2, width >> len(axes_a), ways * width), shape(count, width), shape(1, width, dtype=f32)]
    outs = pl.pallas_call(
        functools.partial(unpack_kernel, ways, offsets),
        out_shape=[shape(size, ways * width)] * offsets + each * (ways - 1),
        compiler_params=params(),
        cost_estimate=pl.CostEstimate(flops=6000000 * 1000, bytes_accessed=4 * 1024 * 1024, transcendentals=0),
        name="unpack",
    )(halo_rows, nodes, *messages)
    return (outs[:offsets], *(outs[offsets + i :: 3] for i in range(3)))


def gather_shares(piece, axes):
    pieces = [piece]
    for axis in axes:
        pieces = pieces + [swapped(p, axis) for p in pieces]
    return pieces


def assemble_kernel(axes, *refs):
    pieces, out = refs[:-1], refs[-1]
    share = share_index(axes)
    rows = pieces[0].shape[1]
    for m, piece in enumerate(pieces):
        start = pl.multiple_of((share ^ m) * rows, rows)
        for part in range(out.shape[0]):
            out[part, pl.ds(start, rows), :] = piece[part]


def assemble(pieces, axes):
    parts, rows, channels = pieces[0].shape
    return pl.pallas_call(
        functools.partial(assemble_kernel, axes),
        out_shape=shape(parts, rows * len(pieces), channels),
        compiler_params=params(),
        name="assemble",
    )(*pieces)


def split_rows(slot_count, ways):
    tiles = slot_count // (ways * TILE)
    first = -(-tiles // 3)
    second = (tiles - first + 1) // 2
    return [size * TILE for size in (first, second, tiles - first - second) if size]


def starts_of(sizes):
    return [sum(sizes[:k]) for k in range(len(sizes))]


def edge_kernel(ways, before, mine, counts, sender_ref, slot_ref, *refs):
    refs = list(refs)

    def take(count):
        taken = refs[:count]
        del refs[:count]
        return taken

    own, nodes, gains, halos = take(ways), take(ways), take(ways), take(2 * RADIUS)
    w_in, w_out = take(2)
    others_a, others_b = take(ways - 1), take(ways - 1)
    outs = refs
    width = own[0].shape[1]
    channels = ways * width
    me = lax.axis_index("chan")
    first = pl.multiple_of(me * (own[0].shape[0] // ways) + before, TILE)
    edges = [own[0][pl.ds(first, mine), :]] + [e[before : before + mine, :] for e in own[1:]]
    local_nodes = nodes[0].shape[0]
    halo_count = sum(h.shape[0] for h in halos)
    to_sender = onehot(column(sender_ref[:, pl.ds(first, mine)]), local_nodes)
    to_slot = onehot(column(slot_ref[:, pl.ds(first, mine)]), local_nodes + halo_count)
    table = jnp.concatenate([h[...] for h in halos], axis=0)
    preact = None
    for d in range(ways):
        if d == 0:
            weights = (w_in[0], w_in[1], w_in[2])
        else:
            weights = (others_a[d - 1][0], others_a[d - 1][1], others_b[d - 1][0])
        sent = dot(to_sender, nodes[d][...]).astype(bf16)
        got = dot(to_slot[:, :local_nodes], nodes[d][...])
        got = (got + dot(to_slot[:, local_nodes:], table[:, d * width : (d + 1) * width])).astype(bf16)
        term = dot(edges[d], weights[0]) + dot(sent, weights[1]) + dot(got, weights[2])
        preact = term if preact is None else preact + term
    hidden = (preact / (1.0 + jnp.exp(-preact))).astype(bf16)
    projected = [dot(hidden, w_out[...])]
    for d in range(1, ways):
        blocks = [slice(h * width, (h + 1) * width) for h in range(ways)]
        projected.append(sum(dot(hidden[:, b], others_b[d - 1][1, :, b]) for b in blocks))
    mean = sum(jnp.sum(p, axis=1, keepdims=True) for p in projected) / channels
    square = sum(jnp.sum(p * p, axis=1, keepdims=True) for p in projected) / channels
    scale = lax.rsqrt(square - mean * mean + 1e-05)
    part = lax.axis_index("dom") * lax.axis_size("rep") + lax.axis_index("rep")
    live_rows = TILE * counts[part] - first
    live = lax.broadcasted_iota(i32, (mine, width), 0) < live_rows
    for d in range(ways):
        normed = (projected[d] - mean) * scale * gains[d][...]
        outs[d][...] = jnp.where(live, (edges[d].astype(f32) + normed).astype(bf16), edges[d])


def edge_update(k, before, mine, counts, senders, slots, edges, nodes, gains, halos, w_in, w_out, others_a, others_b):
    ways = len(nodes)
    width = edges[0].shape[1]
    channels = ways * width
    operands = [*edges, *nodes, *gains, *halos, w_in, w_out, *others_a, *others_b]
    return pl.pallas_call(
        functools.partial(edge_kernel, ways, before, mine),
        out_shape=[shape(mine, width)] * ways,
        in_specs=[SMEM] + [VMEM] * (2 + len(operands)),
        out_specs=[VMEM] * ways,
        compiler_params=params(),
        cost_estimate=pl.CostEstimate(
            flops=2 * mine * channels * (4 * channels + 768),
            bytes_accessed=8 * channels * channels,
            transcendentals=mine * channels,
        ),
        name=f"edge_update_{k}",
    )(counts, senders, slots, *operands)


def collect_kernel(ways, places, local_nodes, last, counts, slot_ref, *refs):
    refs = list(refs)
    parts = [refs.pop(0) for _ in places]
    sums = refs.pop(0)[...] if len(refs) > (1 + 2 * RADIUS if last else 1) else None
    me = lax.axis_index("chan")
    part = lax.axis_index("dom") * lax.axis_size("rep") + lax.axis_index("rep")
    live_rows = TILE * counts[part]
    whole = slot_ref.shape[1] // ways
    table_rows = refs[0].shape[0] + (sum(r.shape[0] for r in refs[1:]) if last else 0)
    for (d, before), block in zip(places, parts):
        mine = block.shape[0]
        first = pl.multiple_of(lax.rem(me + d, ways) * whole + before, TILE)
        slots = slot_ref[:, pl.ds(first, mine)]
        ids = first + lax.broadcasted_iota(i32, (1, mine), 1)
        slots = jnp.where(ids < live_rows, slots, -1)
        rows = lax.broadcasted_iota(i32, (table_rows, mine), 0)
        hits = (rows == jnp.broadcast_to(slots, (table_rows, mine))).astype(f32).astype(bf16)
        term = dot(hits, block[...])
        sums = term if sums is None else sums + term
    if not last:
        refs[0][...] = sums
        return
    refs[0][...] = sums[:local_nodes]
    start = local_nodes
    for out in refs[1:]:
        size = out.shape[0]
        out[...] = sums[start : start + size].astype(bf16)
        start += size


def collect(places, parts, sums, counts, slots, ways, local_nodes, halo_size, last):
    width = parts[0].shape[1]
    table_rows = local_nodes + 2 * RADIUS * halo_size
    before = [] if sums is None else [sums]
    if last:
        outs = [shape(local_nodes, width, dtype=f32)] + [shape(halo_size, width)] * (2 * RADIUS)
    else:
        outs = [shape(table_rows, width, dtype=f32)]
    return pl.pallas_call(
        functools.partial(collect_kernel, ways, places, local_nodes, last),
        out_shape=outs,
        in_specs=[SMEM] + [VMEM] * (1 + len(parts) + len(before)),
        out_specs=[VMEM] * len(outs),
        compiler_params=params(),
        name="collect",
    )(counts, slots, *parts, *before)


def finish_kernel(rows_ref, own, *refs):
    returned, out = refs[:-1], refs[-1]
    total = own[...]
    for j, rows in enumerate(returned):
        size = rows.shape[0]
        ids = lax.broadcasted_iota(i32, (own.shape[0], size), 0)
        hits = (ids == jnp.broadcast_to(rows_ref[0, j : j + 1, :], ids.shape)).astype(f32).astype(bf16)
        total = total + dot(hits, rows[...])
    out[...] = total


def finish(halo_rows, own, returned):
    return pl.pallas_call(
        finish_kernel,
        out_shape=shape(*own.shape, dtype=f32),
        compiler_params=params(),
        name="finish",
    )(halo_rows, own, *returned)


def local(
    node_feats,
    edge_feats,
    senders,
    receiver_slot,
    halo_rows,
    tile_counts,
    weight_in,
    weight_out,
    norm_gain,
):
    ways = lax.axis_size("chan")
    me = lax.axis_index("chan")
    offsets = [shift_by for shift_by in range(-RADIUS, RADIUS + 1) if shift_by != 0]
    local_nodes, width = node_feats.shape
    halo_size = halo_rows.shape[2]
    slot_count = edge_feats.shape[0]
    sizes = split_rows(slot_count, ways)
    whole = slot_count // ways
    distances = range(1, ways)
    axes_a, axes_b = even(SHARERS_A), even(SHARERS_B)

    gain = norm_gain.reshape(1, width)
    sender_row, slot_row = senders.reshape(1, -1), receiver_slot.reshape(1, -1)
    message_a, message_b = prepare_shares(weight_in, weight_out, node_feats, gain, ways, axes_a, axes_b)
    blocks = prepare_blocks(edge_feats, ways)
    blocks = [tie(block, sender_row, slot_row) for block in blocks]
    crossed_a = [shifted(message_a, "chan", d) for d in distances]
    crossed_b = [shifted(message_b, "chan", d) for d in distances]
    outgoing, pieces, nodes, gains = unpack(halo_rows, node_feats, crossed_a, ways, axes_a)
    nodes, gains = [node_feats, *nodes], [gain, *gains]
    halos = [shifted(rows, ("dom", "rep"), by) for rows, by in zip(outgoing, offsets)]
    edges = [edge_feats] + [shifted(blocks[d - 1], "chan", d) for d in distances]
    crossed_b = [tie(piece, *halos) for piece in crossed_b]
    others_a = [assemble(gather_shares(piece, axes_a), axes_a) for piece in pieces]
    others_b = [assemble(gather_shares(piece, axes_b), axes_b) for piece in crossed_b]

    def collected(places, parts, sums, last=False):
        return collect(places, parts, sums, tile_counts, slot_row, ways, local_nodes, halo_size, last)

    finished = jnp.zeros((slot_count, width), bf16)
    kept, arrived = [], []
    for k, (before, mine) in enumerate(zip(starts_of(sizes), sizes)):
        parts = edge_update(
            k, before, mine, tile_counts, sender_row, slot_row, edges, nodes, gains, halos,
            weight_in, weight_out, others_a, others_b,
        )
        edges[0] = tie(edges[0], *parts)
        kept.append(parts[0])
        arrived.append([shifted(parts[d], "chan", -d) for d in distances])
        for d, part in enumerate([parts[0], *arrived[-1]]):
            first = ((me + d) % ways) * whole + before
            finished = lax.dynamic_update_slice_in_dim(finished, part, first, 0)
    starts = starts_of(sizes)
    (sums,) = collected([(0, b) for b in starts], kept, None)
    for k in range(len(sizes) - 1):
        (sums,) = collected([(d, starts[k]) for d in distances], arrived[k], sums)
    own, *pieces = collected([(d, starts[-1]) for d in distances], arrived[-1], sums, True)
    returned = [shifted(piece, ("dom", "rep"), -by) for piece, by in zip(pieces, offsets)]
    return (finished, finish(halo_rows, own, returned))


def solution(mesh):
    placed = (
        P(("groups", "dom", "rep"), "chan"),
        P(("groups", "dom", "rep"), "chan"),
        P(("groups", "dom", "rep")),
        P(("groups", "dom", "rep")),
        P(("groups", "dom", "rep"), None, None),
        P("groups"),
        P(None, "chan", None),
        P(None, "chan"),
        P("chan"),
    )
    return jax.shard_map(
        local,
        mesh=mesh,
        in_specs=placed,
        out_specs=(P(("groups", "dom", "rep"), "chan"), P(("groups", "dom", "rep"), "chan")),
        check_vma=False,
    )
```

```python
import functools

import jax
import jax.numpy as jnp
from jax import lax
from jax.experimental import pallas as pl
from jax.experimental.pallas import tpu as pltpu
from jax.sharding import PartitionSpec as P

TILE = 128
RADIUS = 2
GAIN_ROWS = 16
SHARERS_A = ("groups", "dom", "rep")
SHARERS_B = ("groups", "rep")
bf16 = jnp.bfloat16
f32 = jnp.float32
i32 = jnp.int32
VMEM_BYTES = 24 * 1024 * 1024
PREPARE_VMEM_BYTES = 60 * 1024 * 1024
HBM = pl.BlockSpec(memory_space=pltpu.HBM)
VMEM = pl.BlockSpec(memory_space=pltpu.VMEM)
SMEM = pl.BlockSpec(memory_space=pltpu.SMEM)


def shape(*dims, dtype=bf16):
    return jax.ShapeDtypeStruct(dims, dtype)


def params(vmem=VMEM_BYTES):
    return pltpu.CompilerParams(vmem_limit_bytes=vmem)


def shifted(block, axis, distance):
    size = lax.axis_size(axis)
    return lax.ppermute(block, axis, [(i, (i + distance) % size) for i in range(size)])


def swapped(block, axis):
    size = lax.axis_size(axis)
    return lax.ppermute(block, axis, [(i, i ^ 1) for i in range(size)])


def even(axes):
    return [axis for axis in axes if lax.axis_size(axis) % 2 == 0]


def share_index(axes):
    return sum((lax.axis_index(axis) % 2) << place for place, axis in enumerate(axes))


def tie(array, *others):
    return lax.optimization_barrier((array, *others))[0]


def dot(a, b):
    return jnp.dot(a, b, preferred_element_type=f32)


def column(row):
    return jnp.transpose(jnp.broadcast_to(row, (128, row.shape[1])))


def onehot(ids, count):
    lanes = lax.broadcasted_iota(i32, ids.shape, 1)
    hits = [(ids == lanes + base).astype(f32).astype(bf16) for base in range(0, count, 128)]
    return jnp.concatenate(hits, axis=1) if len(hits) > 1 else hits[0]


def copier(sems):
    copies = []

    def copy(source, target):
        copies.append(pltpu.make_async_copy(source, target, sems.at[len(copies)]))
        copies[-1].start()

    def finish():
        for c in copies:
            c.wait()

    return copy, finish


def first_kernel(axes, w_in, nodes, gain, packed, first, sems):
    copy, finish = copier(sems)
    count, width = nodes.shape
    rows = width >> len(axes)
    start = pl.multiple_of(share_index(axes) * rows, rows)
    for part in range(2):
        copy(w_in.at[part, pl.ds(start, rows), :], first.at[part])
    copy(nodes, packed.at[pl.ds(0, count), :])
    high = gain[...].astype(bf16)
    middle = (gain[...] - high.astype(f32)).astype(bf16)
    low = (gain[...] - high.astype(f32) - middle.astype(f32)).astype(bf16)
    row_ids = lax.broadcasted_iota(i32, (GAIN_ROWS, width), 0)
    rows = jnp.where(row_ids == 0, high.astype(f32), 0.0)
    rows = jnp.where(row_ids == 1, middle.astype(f32), rows)
    rows = jnp.where(row_ids == 2, low.astype(f32), rows)
    packed[count:, :] = rows.astype(bf16)
    finish()


def prepare_first(weight_in, nodes, gain, ways, axes):
    count, width = nodes.shape
    return pl.pallas_call(
        functools.partial(first_kernel, axes),
        out_shape=[shape(count + GAIN_ROWS, width), shape(2, width >> len(axes), ways * width)],
        in_specs=[HBM, HBM, VMEM],
        out_specs=[VMEM] * 2,
        scratch_shapes=[pltpu.SemaphoreType.DMA((3,))],
        compiler_params=params(PREPARE_VMEM_BYTES),
        name="prepare_first",
    )(weight_in, nodes, gain)


def second_kernel(ways, axes, w_in, w_out, second, sems):
    copy, finish = copier(sems)
    width = w_out.shape[1]
    rows = width >> len(axes)
    start = pl.multiple_of(share_index(axes) * rows, rows)
    copy(w_in.at[2, pl.ds(start, rows), :], second.at[0])
    for h in range(ways):
        copy(w_out.at[pl.ds(h * width + start, rows), :], second.at[1, :, pl.ds(h * width, width)])
    finish()


def prepare_second(weight_in, weight_out, ways, axes):
    width = weight_out.shape[1]
    return pl.pallas_call(
        functools.partial(second_kernel, ways, axes),
        out_shape=shape(2, width >> len(axes), ways * width),
        in_specs=[HBM, HBM],
        out_specs=VMEM,
        scratch_shapes=[pltpu.SemaphoreType.DMA((1 + ways,))],
        compiler_params=params(PREPARE_VMEM_BYTES),
        name="prepare_second",
    )(weight_in, weight_out)


def block_kernel(ways, edges, *rest):
    blocks, sems = rest[:-1], rest[-1]
    copy, finish = copier(sems)
    me = lax.axis_index("chan")
    mine = edges.shape[0] // ways
    for d in range(1, ways):
        row = pl.multiple_of(lax.rem(me + d, ways) * mine, TILE)
        copy(edges.at[pl.ds(row, mine), :], blocks[d - 1])
    finish()


def prepare_blocks(edge_feats, ways):
    slot_count, width = edge_feats.shape
    return pl.pallas_call(
        functools.partial(block_kernel, ways),
        out_shape=[shape(slot_count // ways, width)] * (ways - 1),
        in_specs=[HBM],
        out_specs=[VMEM] * (ways - 1),
        scratch_shapes=[pltpu.SemaphoreType.DMA((ways - 1,))],
        compiler_params=params(),
        name="prepare_blocks",
    )(edge_feats)


def unpack_kernel(ways, halo_count, rows_ref, nodes, *refs):
    messages, outs = refs[: ways - 1], list(refs[ways - 1 :])
    halos = [outs.pop(0) for _ in range(halo_count)]
    others, gains = outs[::2], outs[1::2]
    count, width = nodes.shape
    for d in range(1, ways):
        message = messages[d - 1]
        others[d - 1][...] = message[:count, :]
        parts = message[count:, :].astype(f32)
        gains[d - 1][...] = parts[0:1, :] + parts[1:2, :] + parts[2:3, :]
    for j in range(halo_count):
        hits = onehot(column(rows_ref[0, j : j + 1, :]), count)
        for d in range(ways):
            table = nodes[...] if d == 0 else others[d - 1][...]
            halos[j][:, d * width : (d + 1) * width] = dot(hits, table).astype(bf16)


def unpack(halo_rows, nodes, messages, ways):
    _, offsets, size = halo_rows.shape
    count, width = nodes.shape
    each = [shape(count, width), shape(1, width, dtype=f32)]
    outs = pl.pallas_call(
        functools.partial(unpack_kernel, ways, offsets),
        out_shape=[shape(size, ways * width)] * offsets + each * (ways - 1),
        compiler_params=params(),
        cost_estimate=pl.CostEstimate(flops=6000000 * 1000, bytes_accessed=4 * 1024 * 1024, transcendentals=0),
        name="unpack",
    )(halo_rows, nodes, *messages)
    return outs[:offsets], outs[offsets::2], outs[offsets + 1 :: 2]


def join_kernel(first, second, out):
    rows = first.shape[1]
    out[:, :rows, :] = first[...]
    out[:, rows:, :] = second[...]


def join(first, second):
    parts, rows, channels = first.shape
    return pl.pallas_call(
        join_kernel,
        out_shape=shape(parts, 2 * rows, channels),
        compiler_params=params(),
        name="join",
    )(first, second)


def gather_shares(piece, axes, waits):
    pieces = [piece]
    for axis in axes:
        if axis == "rep":
            pieces[-1] = tie(pieces[-1], *waits)
        pieces = pieces + [swapped(p, axis) for p in pieces]
    return pieces


def assemble_kernel(axes, *refs):
    pieces, out = refs[:-1], refs[-1]
    share = share_index(axes)
    each = (1 << len(axes)) // len(pieces)
    rows = pieces[0].shape[1] // each
    for m in range(len(pieces) * each):
        start = pl.multiple_of((share ^ m) * rows, rows)
        place = m % each * rows
        for part in range(out.shape[0]):
            out[part, pl.ds(start, rows), :] = pieces[m // each][part, place : place + rows, :]


def assemble(pieces, axes):
    parts, rows, channels = pieces[0].shape
    return pl.pallas_call(
        functools.partial(assemble_kernel, axes),
        out_shape=shape(parts, rows * len(pieces), channels),
        compiler_params=params(),
        name="assemble",
    )(*pieces)


def split_rows(slot_count, ways):
    tiles = slot_count // (ways * TILE)
    first = -(-tiles // 3)
    second = (tiles - first + 1) // 2
    return [size * TILE for size in (first, second, tiles - first - second) if size]


def starts_of(sizes):
    return [sum(sizes[:k]) for k in range(len(sizes))]


def edge_kernel(ways, before, mine, counts, sender_ref, slot_ref, *refs):
    refs = list(refs)

    def take(count):
        taken = refs[:count]
        del refs[:count]
        return taken

    own, nodes, gains, halos = take(ways), take(ways), take(ways), take(2 * RADIUS)
    w_in, w_out = take(2)
    others_a, others_b = take(ways - 1), take(ways - 1)
    outs = refs
    width = own[0].shape[1]
    channels = ways * width
    me = lax.axis_index("chan")
    first = pl.multiple_of(me * (own[0].shape[0] // ways) + before, TILE)
    edges = [own[0][pl.ds(first, mine), :]] + [e[before : before + mine, :] for e in own[1:]]
    local_nodes = nodes[0].shape[0]
    halo_count = sum(h.shape[0] for h in halos)
    to_sender = onehot(column(sender_ref[:, pl.ds(first, mine)]), local_nodes)
    to_slot = onehot(column(slot_ref[:, pl.ds(first, mine)]), local_nodes + halo_count)
    table = jnp.concatenate([h[...] for h in halos], axis=0)
    preact = None
    for d in range(ways):
        if d == 0:
            weights = (w_in[0], w_in[1], w_in[2])
        else:
            weights = (others_a[d - 1][0], others_a[d - 1][1], others_b[d - 1][0])
        sent = dot(to_sender, nodes[d][...]).astype(bf16)
        got = dot(to_slot[:, :local_nodes], nodes[d][...])
        got = (got + dot(to_slot[:, local_nodes:], table[:, d * width : (d + 1) * width])).astype(bf16)
        term = dot(edges[d], weights[0]) + dot(sent, weights[1]) + dot(got, weights[2])
        preact = term if preact is None else preact + term
    hidden = (preact / (1.0 + jnp.exp(-preact))).astype(bf16)
    projected = [dot(hidden, w_out[...])]
    for d in range(1, ways):
        blocks = [slice(h * width, (h + 1) * width) for h in range(ways)]
        projected.append(sum(dot(hidden[:, b], others_b[d - 1][1, :, b]) for b in blocks))
    mean = sum(jnp.sum(p, axis=1, keepdims=True) for p in projected) / channels
    square = sum(jnp.sum(p * p, axis=1, keepdims=True) for p in projected) / channels
    scale = lax.rsqrt(square - mean * mean + 1e-05)
    part = lax.axis_index("dom") * lax.axis_size("rep") + lax.axis_index("rep")
    live_rows = TILE * counts[part] - first
    live = lax.broadcasted_iota(i32, (mine, width), 0) < live_rows
    for d in range(ways):
        normed = (projected[d] - mean) * scale * gains[d][...]
        outs[d][...] = jnp.where(live, (edges[d].astype(f32) + normed).astype(bf16), edges[d])


def edge_update(k, before, mine, counts, senders, slots, edges, nodes, gains, halos, w_in, w_out, others_a, others_b):
    ways = len(nodes)
    width = edges[0].shape[1]
    channels = ways * width
    operands = [*edges, *nodes, *gains, *halos, w_in, w_out, *others_a, *others_b]
    return pl.pallas_call(
        functools.partial(edge_kernel, ways, before, mine),
        out_shape=[shape(mine, width)] * ways,
        in_specs=[SMEM] + [VMEM] * (2 + len(operands)),
        out_specs=[VMEM] * ways,
        compiler_params=params(),
        cost_estimate=pl.CostEstimate(
            flops=2 * mine * channels * (4 * channels + 768),
            bytes_accessed=8 * channels * channels,
            transcendentals=mine * channels,
        ),
        name=f"edge_update_{k}",
    )(counts, senders, slots, *operands)


def collect_kernel(ways, places, local_nodes, last, counts, slot_ref, *refs):
    refs = list(refs)
    parts = [refs.pop(0) for _ in places]
    sums = refs.pop(0)[...] if len(refs) > (1 + 2 * RADIUS if last else 1) else None
    me = lax.axis_index("chan")
    part = lax.axis_index("dom") * lax.axis_size("rep") + lax.axis_index("rep")
    live_rows = TILE * counts[part]
    whole = slot_ref.shape[1] // ways
    table_rows = refs[0].shape[0] + (sum(r.shape[0] for r in refs[1:]) if last else 0)
    for (d, before), block in zip(places, parts):
        mine = block.shape[0]
        first = pl.multiple_of(lax.rem(me + d, ways) * whole + before, TILE)
        slots = slot_ref[:, pl.ds(first, mine)]
        ids = first + lax.broadcasted_iota(i32, (1, mine), 1)
        slots = jnp.where(ids < live_rows, slots, -1)
        rows = lax.broadcasted_iota(i32, (table_rows, mine), 0)
        hits = (rows == jnp.broadcast_to(slots, (table_rows, mine))).astype(f32).astype(bf16)
        term = dot(hits, block[...])
        sums = term if sums is None else sums + term
    if not last:
        refs[0][...] = sums
        return
    refs[0][...] = sums[:local_nodes]
    start = local_nodes
    for out in refs[1:]:
        size = out.shape[0]
        out[...] = sums[start : start + size].astype(bf16)
        start += size


def collect(places, parts, sums, counts, slots, ways, local_nodes, halo_size, last):
    width = parts[0].shape[1]
    table_rows = local_nodes + 2 * RADIUS * halo_size
    before = [] if sums is None else [sums]
    if last:
        outs = [shape(local_nodes, width, dtype=f32)] + [shape(halo_size, width)] * (2 * RADIUS)
    else:
        outs = [shape(table_rows, width, dtype=f32)]
    return pl.pallas_call(
        functools.partial(collect_kernel, ways, places, local_nodes, last),
        out_shape=outs,
        in_specs=[SMEM] + [VMEM] * (1 + len(parts) + len(before)),
        out_specs=[VMEM] * len(outs),
        compiler_params=params(),
        name="collect",
    )(counts, slots, *parts, *before)


def finish_kernel(rows_ref, own, *refs):
    returned, out = refs[:-1], refs[-1]
    total = own[...]
    for j, rows in enumerate(returned):
        size = rows.shape[0]
        ids = lax.broadcasted_iota(i32, (own.shape[0], size), 0)
        hits = (ids == jnp.broadcast_to(rows_ref[0, j : j + 1, :], ids.shape)).astype(f32).astype(bf16)
        total = total + dot(hits, rows[...])
    out[...] = total


def finish(halo_rows, own, returned):
    return pl.pallas_call(
        finish_kernel,
        out_shape=shape(*own.shape, dtype=f32),
        compiler_params=params(),
        name="finish",
    )(halo_rows, own, *returned)


def local(
    node_feats,
    edge_feats,
    senders,
    receiver_slot,
    halo_rows,
    tile_counts,
    weight_in,
    weight_out,
    norm_gain,
):
    ways = lax.axis_size("chan")
    me = lax.axis_index("chan")
    offsets = [shift_by for shift_by in range(-RADIUS, RADIUS + 1) if shift_by != 0]
    local_nodes, width = node_feats.shape
    halo_size = halo_rows.shape[2]
    slot_count = edge_feats.shape[0]
    sizes = split_rows(slot_count, ways)
    whole = slot_count // ways
    distances = range(1, ways)
    axes_a, axes_b = even(SHARERS_A), even(SHARERS_B)

    gain = norm_gain.reshape(1, width)
    sender_row, slot_row = senders.reshape(1, -1), receiver_slot.reshape(1, -1)
    packed, message_a = prepare_first(weight_in, node_feats, gain, ways, axes_a)
    message_b = prepare_second(weight_in, weight_out, ways, axes_b)
    blocks = prepare_blocks(edge_feats, ways)
    blocks = [tie(block, sender_row, slot_row) for block in blocks]
    received = [shifted(packed, "chan", d) for d in distances]
    crossed_a = [shifted(message_a, "chan", d) for d in distances]
    crossed_b = [shifted(message_b, "chan", d) for d in distances]
    outgoing, nodes, gains = unpack(halo_rows, node_feats, received, ways)
    nodes, gains = [node_feats, *nodes], [gain, *gains]
    halos = [shifted(rows, ("dom", "rep"), by) for rows, by in zip(outgoing, offsets)]
    edges = [edge_feats] + [shifted(blocks[d - 1], "chan", d) for d in distances]
    pieces = [tie(piece, *halos[:3]) for piece in crossed_a]
    pieces = [join(piece, swapped(piece, axes_a[0])) for piece in pieces]
    pieces = [tie(piece, *halos[3:]) for piece in pieces]
    crossed_b = [tie(piece, *pieces) for piece in crossed_b]
    others_a = [assemble(gather_shares(piece, axes_a[1:], edges[1:]), axes_a) for piece in pieces]
    others_b = [assemble(gather_shares(piece, axes_b, ()), axes_b) for piece in crossed_b]

    def collected(places, parts, sums, last=False):
        return collect(places, parts, sums, tile_counts, slot_row, ways, local_nodes, halo_size, last)

    finished = jnp.zeros((slot_count, width), bf16)
    kept, arrived = [], []
    for k, (before, mine) in enumerate(zip(starts_of(sizes), sizes)):
        parts = edge_update(
            k, before, mine, tile_counts, sender_row, slot_row, edges, nodes, gains, halos,
            weight_in, weight_out, others_a, others_b,
        )
        edges[0] = tie(edges[0], *parts)
        kept.append(parts[0])
        arrived.append([shifted(parts[d], "chan", -d) for d in distances])
        for d, part in enumerate([parts[0], *arrived[-1]]):
            first = ((me + d) % ways) * whole + before
            finished = lax.dynamic_update_slice_in_dim(finished, part, first, 0)
    starts = starts_of(sizes)
    (sums,) = collected([(0, b) for b in starts], kept, None)
    for k in range(len(sizes) - 1):
        (sums,) = collected([(d, starts[k]) for d in distances], arrived[k], sums)
    own, *pieces = collected([(d, starts[-1]) for d in distances], arrived[-1], sums, True)
    returned = [shifted(piece, ("dom", "rep"), -by) for piece, by in zip(pieces, offsets)]
    return (finished, finish(halo_rows, own, returned))


def solution(mesh):
    placed = (
        P(("groups", "dom", "rep"), "chan"),
        P(("groups", "dom", "rep"), "chan"),
        P(("groups", "dom", "rep")),
        P(("groups", "dom", "rep")),
        P(("groups", "dom", "rep"), None, None),
        P("groups"),
        P(None, "chan", None),
        P(None, "chan"),
        P("chan"),
    )
    return jax.shard_map(
        local,
        mesh=mesh,
        in_specs=placed,
        out_specs=(P(("groups", "dom", "rep"), "chan"), P(("groups", "dom", "rep"), "chan")),
        check_vma=False,
    )
```

```python
import functools

import jax
import jax.numpy as jnp
from jax import lax
from jax.experimental import pallas as pl
from jax.experimental.pallas import tpu as pltpu
from jax.sharding import PartitionSpec as P

TILE = 128
RADIUS = 2
GAIN_ROWS = 16
SHARERS_A = ("groups", "dom", "rep")
SHARERS_B = ("groups", "rep")
bf16 = jnp.bfloat16
f32 = jnp.float32
i32 = jnp.int32
VMEM_BYTES = 24 * 1024 * 1024
PREPARE_VMEM_BYTES = 60 * 1024 * 1024
HBM = pl.BlockSpec(memory_space=pltpu.HBM)
VMEM = pl.BlockSpec(memory_space=pltpu.VMEM)
SMEM = pl.BlockSpec(memory_space=pltpu.SMEM)


def shape(*dims, dtype=bf16):
    return jax.ShapeDtypeStruct(dims, dtype)


def params(vmem=VMEM_BYTES):
    return pltpu.CompilerParams(vmem_limit_bytes=vmem)


def shifted(block, axis, distance):
    size = lax.axis_size(axis)
    return lax.ppermute(block, axis, [(i, (i + distance) % size) for i in range(size)])


def swapped(block, axis):
    size = lax.axis_size(axis)
    return lax.ppermute(block, axis, [(i, i ^ 1) for i in range(size)])


def even(axes):
    return [axis for axis in axes if lax.axis_size(axis) % 2 == 0]


def share_index(axes):
    return sum((lax.axis_index(axis) % 2) << place for place, axis in enumerate(axes))


def tie(array, *others):
    return lax.optimization_barrier((array, *others))[0]


def dot(a, b):
    return jnp.dot(a, b, preferred_element_type=f32)


def column(row):
    return jnp.transpose(jnp.broadcast_to(row, (128, row.shape[1])))


def onehot(ids, count):
    lanes = lax.broadcasted_iota(i32, ids.shape, 1)
    hits = [(ids == lanes + base).astype(f32).astype(bf16) for base in range(0, count, 128)]
    return jnp.concatenate(hits, axis=1) if len(hits) > 1 else hits[0]


def copier(sems):
    copies = []

    def copy(source, target):
        copies.append(pltpu.make_async_copy(source, target, sems.at[len(copies)]))
        copies[-1].start()

    def finish():
        for c in copies:
            c.wait()

    return copy, finish


def first_kernel(axes, w_in, first, sems):
    copy, finish = copier(sems)
    rows = w_in.shape[1] >> len(axes)
    start = pl.multiple_of(share_index(axes) * rows, rows)
    for part in range(2):
        copy(w_in.at[part, pl.ds(start, rows), :], first.at[part])
    finish()


def prepare_first(weight_in, axes):
    _, width, channels = weight_in.shape
    return pl.pallas_call(
        functools.partial(first_kernel, axes),
        out_shape=shape(2, width >> len(axes), channels),
        in_specs=[HBM],
        out_specs=VMEM,
        scratch_shapes=[pltpu.SemaphoreType.DMA((2,))],
        compiler_params=params(PREPARE_VMEM_BYTES),
        name="prepare_first",
    )(weight_in)


def second_kernel(ways, axes, w_in, w_out, second, sems):
    copy, finish = copier(sems)
    width = w_out.shape[1]
    rows = width >> len(axes)
    start = pl.multiple_of(share_index(axes) * rows, rows)
    copy(w_in.at[2, pl.ds(start, rows), :], second.at[0])
    for h in range(ways):
        copy(w_out.at[pl.ds(h * width + start, rows), :], second.at[1, :, pl.ds(h * width, width)])
    finish()


def prepare_second(weight_in, weight_out, ways, axes):
    width = weight_out.shape[1]
    return pl.pallas_call(
        functools.partial(second_kernel, ways, axes),
        out_shape=shape(2, width >> len(axes), ways * width),
        in_specs=[HBM, HBM],
        out_specs=VMEM,
        scratch_shapes=[pltpu.SemaphoreType.DMA((1 + ways,))],
        compiler_params=params(PREPARE_VMEM_BYTES),
        name="prepare_second",
    )(weight_in, weight_out)


def gain_terms(gain, width):
    high = gain.astype(bf16)
    middle = (gain - high.astype(f32)).astype(bf16)
    low = (gain - high.astype(f32) - middle.astype(f32)).astype(bf16)
    row_ids = lax.broadcasted_iota(i32, (GAIN_ROWS, width), 0)
    rows = jnp.where(row_ids == 0, high.astype(f32), 0.0)
    rows = jnp.where(row_ids == 1, middle.astype(f32), rows)
    return jnp.where(row_ids == 2, low.astype(f32), rows).astype(bf16)


def block_kernel(ways, split, early, edges, gain, *rest):
    blocks, sems = rest[:-1], rest[-1]
    copy, finish = copier(sems)
    me = lax.axis_index("chan")
    width = edges.shape[1]
    for d in range(1, ways):
        row = pl.multiple_of(lax.rem(me + d, ways) * split, TILE)
        copy(edges.at[pl.ds(row, split), :], blocks[d - 1].at[pl.ds(0, split), :])
        if early:
            copy(edges.at[pl.ds(ways * split, early), :], blocks[d - 1].at[pl.ds(split, early), :])
        blocks[d - 1][split + early :, :] = gain_terms(gain[...], width)
    if len(blocks) == ways:
        late = blocks[-1].shape[0]
        copy(edges.at[pl.ds(ways * split + early, late), :], blocks[-1])
    finish()


def prepare_blocks(edge_feats, gain, ways, split, early, late):
    width = edge_feats.shape[1]
    outs = [shape(split + early + GAIN_ROWS, width)] * (ways - 1) + [shape(late, width)] * (late > 0)
    copies = (ways - 1) * (2 if early else 1) + (late > 0)
    return pl.pallas_call(
        functools.partial(block_kernel, ways, split, early),
        out_shape=outs,
        in_specs=[HBM, VMEM],
        out_specs=[VMEM] * len(outs),
        scratch_shapes=[pltpu.SemaphoreType.DMA((copies,))],
        compiler_params=params(),
        name="prepare_blocks",
    )(edge_feats, gain)


def halo_kernel(ways, rows_ref, *refs):
    nodes, halos = refs[:ways], refs[ways:]
    count, width = nodes[0].shape
    for j, halo in enumerate(halos):
        hits = onehot(column(rows_ref[0, j : j + 1, :]), count)
        for d in range(ways):
            halo[:, d * width : (d + 1) * width] = dot(hits, nodes[d][...]).astype(bf16)


def halo_gather(halo_rows, nodes):
    ways = len(nodes)
    _, offsets, size = halo_rows.shape
    return pl.pallas_call(
        functools.partial(halo_kernel, ways),
        out_shape=[shape(size, ways * nodes[0].shape[1])] * offsets,
        compiler_params=params(),
        cost_estimate=pl.CostEstimate(flops=6 * 10**9, bytes_accessed=4 * 1024 * 1024, transcendentals=0),
        name="halo_gather",
    )(halo_rows, *nodes)


def join_kernel(first, second, out):
    rows = first.shape[1]
    out[:, :rows, :] = first[...]
    out[:, rows:, :] = second[...]


def join(first, second):
    parts, rows, channels = first.shape
    return pl.pallas_call(
        join_kernel,
        out_shape=shape(parts, 2 * rows, channels),
        compiler_params=params(),
        name="join",
    )(first, second)


def gather_shares(piece, axes, waits):
    pieces = [piece]
    for axis in axes:
        if axis == "rep":
            pieces[-1] = tie(pieces[-1], *waits)
        pieces = pieces + [swapped(p, axis) for p in pieces]
    return pieces


def assemble_kernel(axes, *refs):
    pieces, out = refs[:-1], refs[-1]
    share = share_index(axes)
    each = (1 << len(axes)) // len(pieces)
    rows = pieces[0].shape[1] // each
    for m in range(len(pieces) * each):
        start = pl.multiple_of((share ^ m) * rows, rows)
        place = m % each * rows
        for part in range(out.shape[0]):
            out[part, pl.ds(start, rows), :] = pieces[m // each][part, place : place + rows, :]


def assemble(pieces, axes):
    parts, rows, channels = pieces[0].shape
    return pl.pallas_call(
        functools.partial(assemble_kernel, axes),
        out_shape=shape(parts, rows * len(pieces), channels),
        compiler_params=params(),
        name="assemble",
    )(*pieces)


def stage_kernel(w_in, w_out, inner, outer, sems):
    copy, finish = copier(sems)
    copy(w_in, inner)
    copy(w_out, outer)
    finish()


def stage(weight_in, weight_out):
    return pl.pallas_call(
        stage_kernel,
        out_shape=[shape(*weight_in.shape), shape(*weight_out.shape)],
        in_specs=[HBM] * 2,
        out_specs=[VMEM] * 2,
        scratch_shapes=[pltpu.SemaphoreType.DMA((2,))],
        compiler_params=params(),
        name="stage",
    )(weight_in, weight_out)


def plan_rows(slot_count, ways):
    tiles = slot_count // TILE
    shared = [2, 2] if ways == 2 and tiles >= 8 and tiles % 2 == 0 else []
    alone = (tiles - sum(shared)) // ways
    chunks = [alone - alone // 2, alone // 2]
    return [size * TILE for size in chunks if size], [size * TILE for size in shared]


def starts_of(sizes):
    return [sum(sizes[:k]) for k in range(len(sizes))]


def edge_kernel(ways, place, mine, late, counts, sender_ref, slot_ref, *refs):
    refs = list(refs)

    def take(count):
        taken = refs[:count]
        del refs[:count]
        return taken

    (own, own_gain), mains, others = take(2), take(ways - 1), take(ways - 1 if late else 0)
    nodes, halos = take(ways), take(2 * RADIUS)
    w_in, w_out = take(2)
    others_a, others_b = take(ways - 1), take(ways - 1)
    outs = refs
    width = own.shape[1]
    channels = ways * width
    me = lax.axis_index("chan")
    split, base, start = place
    first = pl.multiple_of(me * split + base, TILE)
    edges = [own[pl.ds(first, mine), :]]
    for d, block in enumerate(mains):
        here = mine - others[d].shape[0] if late else mine
        rows = block[start : start + here, :]
        edges.append(jnp.concatenate([rows, others[d][...]], axis=0) if late else rows)
    local_nodes = nodes[0].shape[0]
    halo_count = sum(h.shape[0] for h in halos)
    to_sender = onehot(column(sender_ref[:, pl.ds(first, mine)]), local_nodes)
    to_slot = onehot(column(slot_ref[:, pl.ds(first, mine)]), local_nodes + halo_count)
    table = jnp.concatenate([h[...] for h in halos], axis=0)
    preact = None
    for d in range(ways):
        if d == 0:
            weights = (w_in[0], w_in[1], w_in[2])
        else:
            weights = (others_a[d - 1][0], others_a[d - 1][1], others_b[d - 1][0])
        sent = dot(to_sender, nodes[d][...]).astype(bf16)
        got = dot(to_slot[:, :local_nodes], nodes[d][...])
        got = (got + dot(to_slot[:, local_nodes:], table[:, d * width : (d + 1) * width])).astype(bf16)
        term = dot(edges[d], weights[0]) + dot(sent, weights[1]) + dot(got, weights[2])
        preact = term if preact is None else preact + term
    hidden = (preact / (1.0 + jnp.exp(-preact))).astype(bf16)
    projected = [dot(hidden, w_out[...])]
    for d in range(1, ways):
        blocks = [slice(h * width, (h + 1) * width) for h in range(ways)]
        projected.append(sum(dot(hidden[:, b], others_b[d - 1][1, :, b]) for b in blocks))
    mean = sum(jnp.sum(p, axis=1, keepdims=True) for p in projected) / channels
    square = sum(jnp.sum(p * p, axis=1, keepdims=True) for p in projected) / channels
    scale = lax.rsqrt(square - mean * mean + 1e-05)
    part = lax.axis_index("dom") * lax.axis_size("rep") + lax.axis_index("rep")
    live_rows = TILE * counts[part] - first
    live = lax.broadcasted_iota(i32, (mine, width), 0) < live_rows
    for d in range(len(outs)):
        if d == 0:
            gain = own_gain[...]
        else:
            terms = mains[d - 1][mains[d - 1].shape[0] - GAIN_ROWS :, :].astype(f32)
            gain = terms[0:1, :] + terms[1:2, :] + terms[2:3, :]
        normed = (projected[d] - mean) * scale * gain
        outs[d][...] = jnp.where(live, (edges[d].astype(f32) + normed).astype(bf16), edges[d])


def edge_update(k, place, mine, results, counts, senders, slots, own, gain, blocks, others, nodes, halos, w_in, w_out, others_a, others_b):
    ways = len(nodes)
    width = own.shape[1]
    channels = ways * width
    operands = [own, gain, *blocks, *others, *nodes, *halos, w_in, w_out, *others_a, *others_b]
    return pl.pallas_call(
        functools.partial(edge_kernel, ways, place, mine, bool(others)),
        out_shape=[shape(mine, width)] * results,
        in_specs=[SMEM] + [VMEM] * (2 + len(operands)),
        out_specs=[VMEM] * results,
        compiler_params=params(),
        cost_estimate=pl.CostEstimate(
            flops=2 * mine * channels * (4 * channels + 768),
            bytes_accessed=8 * channels * channels,
            transcendentals=mine * channels,
        ),
        name=f"edge_update_{k}",
    )(counts, senders, slots, *operands)


def collect_kernel(ways, places, local_nodes, last, counts, slot_ref, *refs):
    refs = list(refs)
    parts = [refs.pop(0) for _ in places]
    sums = refs.pop(0)[...] if len(refs) > (1 + 2 * RADIUS if last else 1) else None
    me = lax.axis_index("chan")
    part = lax.axis_index("dom") * lax.axis_size("rep") + lax.axis_index("rep")
    live_rows = TILE * counts[part]
    table_rows = refs[0].shape[0] + (sum(r.shape[0] for r in refs[1:]) if last else 0)
    for (d, split, base), block in zip(places, parts):
        mine = block.shape[0]
        first = pl.multiple_of(lax.rem(me + d, ways) * split + base, TILE)
        slots = slot_ref[:, pl.ds(first, mine)]
        ids = first + lax.broadcasted_iota(i32, (1, mine), 1)
        slots = jnp.where(ids < live_rows, slots, -1)
        rows = lax.broadcasted_iota(i32, (table_rows, mine), 0)
        hits = (rows == jnp.broadcast_to(slots, (table_rows, mine))).astype(f32).astype(bf16)
        term = dot(hits, block[...])
        sums = term if sums is None else sums + term
    if not last:
        refs[0][...] = sums
        return
    refs[0][...] = sums[:local_nodes]
    start = local_nodes
    for out in refs[1:]:
        size = out.shape[0]
        out[...] = sums[start : start + size].astype(bf16)
        start += size


def collect(places, parts, sums, counts, slots, ways, local_nodes, halo_size, last):
    width = parts[0].shape[1]
    table_rows = local_nodes + 2 * RADIUS * halo_size
    before = [] if sums is None else [sums]
    if last:
        outs = [shape(local_nodes, width, dtype=f32)] + [shape(halo_size, width)] * (2 * RADIUS)
    else:
        outs = [shape(table_rows, width, dtype=f32)]
    return pl.pallas_call(
        functools.partial(collect_kernel, ways, places, local_nodes, last),
        out_shape=outs,
        in_specs=[SMEM] + [VMEM] * (1 + len(parts) + len(before)),
        out_specs=[VMEM] * len(outs),
        compiler_params=params(),
        name="collect",
    )(counts, slots, *parts, *before)


def write_kernel(ways, places, *refs):
    parts, out = refs[:-1], refs[-1]
    me = lax.axis_index("chan")
    for (d, split, base), block in zip(places, parts):
        first = pl.multiple_of(lax.rem(me + d, ways) * split + base, TILE)
        out[pl.ds(first, block.shape[0]), :] = block[...]


def write(places, parts, slot_count, ways):
    return pl.pallas_call(
        functools.partial(write_kernel, ways, places),
        out_shape=shape(slot_count, parts[0].shape[1]),
        compiler_params=params(),
        name="write",
    )(*parts)


def finish_kernel(rows_ref, own, *refs):
    returned, out = refs[:-1], refs[-1]
    total = own[...]
    for j, rows in enumerate(returned):
        size = rows.shape[0]
        ids = lax.broadcasted_iota(i32, (own.shape[0], size), 0)
        hits = (ids == jnp.broadcast_to(rows_ref[0, j : j + 1, :], ids.shape)).astype(f32).astype(bf16)
        total = total + dot(hits, rows[...])
    out[...] = total


def finish(halo_rows, own, returned):
    return pl.pallas_call(
        finish_kernel,
        out_shape=shape(*own.shape, dtype=f32),
        compiler_params=params(),
        name="finish",
    )(halo_rows, own, *returned)


def local(
    node_feats,
    edge_feats,
    senders,
    receiver_slot,
    halo_rows,
    tile_counts,
    weight_in,
    weight_out,
    norm_gain,
):
    ways = lax.axis_size("chan")
    offsets = [shift_by for shift_by in range(-RADIUS, RADIUS + 1) if shift_by != 0]
    local_nodes, width = node_feats.shape
    halo_size = halo_rows.shape[2]
    slot_count = edge_feats.shape[0]
    alone, shared = plan_rows(slot_count, ways)
    split, early, late = sum(alone), sum(shared[:1]), sum(shared[1:])
    distances = range(1, ways)
    axes_a, axes_b = even(SHARERS_A), even(SHARERS_B)

    gain = norm_gain.reshape(1, width)
    sender_row, slot_row = senders.reshape(1, -1), receiver_slot.reshape(1, -1)
    message_a = prepare_first(weight_in, axes_a)
    message_b = prepare_second(weight_in, weight_out, ways, axes_b)
    blocks = prepare_blocks(edge_feats, gain, ways, split, early, late)
    blocks = [tie(block, sender_row, slot_row) for block in blocks]
    nodes = [node_feats] + [shifted(node_feats, "chan", d) for d in distances]
    crossed_a = [shifted(message_a, "chan", d) for d in distances]
    crossed_b = [shifted(message_b, "chan", d) for d in distances]
    outgoing = halo_gather(halo_rows, nodes)
    halos = [shifted(rows, ("dom", "rep"), by) for rows, by in zip(outgoing, offsets)]
    edges = [shifted(blocks[d - 1], "chan", d) for d in distances]
    late_edges = [shifted(blocks[-1], "chan", d) for d in distances if late]
    pieces = [tie(piece, *halos[:3]) for piece in crossed_a]
    pieces = [join(piece, swapped(piece, axes_a[0])) for piece in pieces]
    pieces = [tie(piece, *halos[3:]) for piece in pieces]
    crossed_b = [tie(piece, *pieces) for piece in crossed_b]
    others_a = [assemble(gather_shares(piece, axes_a[1:], edges), axes_a) for piece in pieces]
    inner, outer = stage(tie(weight_in, *outgoing), weight_out)
    others_b = [assemble(gather_shares(piece, axes_b, [inner, outer]), axes_b) for piece in crossed_b]

    def collected(places, parts, sums, last=False):
        return collect(places, parts, sums, tile_counts, slot_row, ways, local_nodes, halo_size, last)

    jobs = [(split, before, before, mine, ways) for before, mine in zip(starts_of(alone), alone)]
    if shared:
        jobs.append((0, ways * split, split, early + late, 1))
    parts, places, order = [], [], edge_feats
    for k, (stride, base, start, mine, results) in enumerate(jobs):
        others = late_edges if k == len(alone) else []
        outs = edge_update(
            k, (stride, base, start), mine, results, tile_counts, sender_row, slot_row, order, gain, edges, others,
            nodes, halos, inner, outer, others_a, others_b,
        )
        order = tie(order, *outs)
        outs = [outs[0]] + [shifted(outs[d], "chan", -d) for d in range(1, results)]
        parts.append(outs)
        places.append([(d, stride, base) for d in range(results)])

    def chosen(which):
        return [places[k][d] for k, d in which], [parts[k][d] for k, d in which]

    count = len(alone)
    final = [(count - 1, d) for d in distances]
    own_parts = [(k, 0) for k in range(len(jobs))]
    (sums,) = collected(*chosen(own_parts), None)
    for k in range(count - 1):
        (sums,) = collected(*chosen([(k, d) for d in distances]), sums)
    own, *pieces = collected(*chosen(final), sums, True)
    returned = [shifted(piece, ("dom", "rep"), -by) for piece, by in zip(pieces, offsets)]
    everything = chosen([(k, d) for k, outs in enumerate(parts) for d in range(len(outs))])
    return (write(*everything, slot_count, ways), finish(halo_rows, own, returned))


def solution(mesh):
    placed = (
        P(("groups", "dom", "rep"), "chan"),
        P(("groups", "dom", "rep"), "chan"),
        P(("groups", "dom", "rep")),
        P(("groups", "dom", "rep")),
        P(("groups", "dom", "rep"), None, None),
        P("groups"),
        P(None, "chan", None),
        P(None, "chan"),
        P("chan"),
    )
    return jax.shard_map(
        local,
        mesh=mesh,
        in_specs=placed,
        out_specs=(P(("groups", "dom", "rep"), "chan"), P(("groups", "dom", "rep"), "chan")),
        check_vma=False,
    )
```

```python
import functools

import jax
import jax.numpy as jnp
from jax import lax
from jax.experimental import pallas as pl
from jax.experimental.pallas import tpu as pltpu
from jax.sharding import PartitionSpec as P

TILE = 128
RADIUS = 2
GAIN_ROWS = 16
SHARERS_A = ("groups", "dom", "rep")
SHARERS_B = ("groups", "rep")
bf16 = jnp.bfloat16
f32 = jnp.float32
i32 = jnp.int32
VMEM_BYTES = 24 * 1024 * 1024
PREPARE_VMEM_BYTES = 60 * 1024 * 1024
HBM = pl.BlockSpec(memory_space=pltpu.HBM)
VMEM = pl.BlockSpec(memory_space=pltpu.VMEM)
SMEM = pl.BlockSpec(memory_space=pltpu.SMEM)


def shape(*dims, dtype=bf16):
    return jax.ShapeDtypeStruct(dims, dtype)


def params(vmem=VMEM_BYTES):
    return pltpu.CompilerParams(vmem_limit_bytes=vmem)


def shifted(block, axis, distance):
    size = lax.axis_size(axis)
    return lax.ppermute(block, axis, [(i, (i + distance) % size) for i in range(size)])


def swapped(block, axis):
    size = lax.axis_size(axis)
    return lax.ppermute(block, axis, [(i, i ^ 1) for i in range(size)])


def even(axes):
    return [axis for axis in axes if lax.axis_size(axis) % 2 == 0]


def share_index(axes):
    return sum((lax.axis_index(axis) % 2) << place for place, axis in enumerate(axes))


def tie(array, *others):
    return lax.optimization_barrier((array, *others))[0]


def dot(a, b):
    return jnp.dot(a, b, preferred_element_type=f32)


def column(row):
    return jnp.transpose(jnp.broadcast_to(row, (128, row.shape[1])))


def onehot(ids, count):
    lanes = lax.broadcasted_iota(i32, ids.shape, 1)
    hits = [(ids == lanes + base).astype(f32).astype(bf16) for base in range(0, count, 128)]
    return jnp.concatenate(hits, axis=1) if len(hits) > 1 else hits[0]


def copier(sems):
    copies = []

    def copy(source, target):
        copies.append(pltpu.make_async_copy(source, target, sems.at[len(copies)]))
        copies[-1].start()

    def finish():
        for c in copies:
            c.wait()

    return copy, finish


def first_kernel(axes, w_in, first, sems):
    copy, finish = copier(sems)
    rows = w_in.shape[1] >> len(axes)
    start = pl.multiple_of(share_index(axes) * rows, rows)
    for part in range(2):
        copy(w_in.at[part, pl.ds(start, rows), :], first.at[part])
    finish()


def prepare_first(weight_in, axes):
    _, width, channels = weight_in.shape
    return pl.pallas_call(
        functools.partial(first_kernel, axes),
        out_shape=shape(2, width >> len(axes), channels),
        in_specs=[HBM],
        out_specs=VMEM,
        scratch_shapes=[pltpu.SemaphoreType.DMA((2,))],
        compiler_params=params(PREPARE_VMEM_BYTES),
        name="prepare_first",
    )(weight_in)


def second_kernel(ways, axes, w_in, w_out, second, sems):
    copy, finish = copier(sems)
    width = w_out.shape[1]
    rows = width >> len(axes)
    start = pl.multiple_of(share_index(axes) * rows, rows)
    copy(w_in.at[2, pl.ds(start, rows), :], second.at[0])
    for h in range(ways):
        copy(w_out.at[pl.ds(h * width + start, rows), :], second.at[1, :, pl.ds(h * width, width)])
    finish()


def prepare_second(weight_in, weight_out, ways, axes):
    width = weight_out.shape[1]
    return pl.pallas_call(
        functools.partial(second_kernel, ways, axes),
        out_shape=shape(2, width >> len(axes), ways * width),
        in_specs=[HBM, HBM],
        out_specs=VMEM,
        scratch_shapes=[pltpu.SemaphoreType.DMA((1 + ways,))],
        compiler_params=params(PREPARE_VMEM_BYTES),
        name="prepare_second",
    )(weight_in, weight_out)


def mask_kernel(counts, slots, out):
    part = lax.axis_index("dom") * lax.axis_size("rep") + lax.axis_index("rep")
    ids = lax.broadcasted_iota(i32, slots.shape, 1)
    out[...] = jnp.where(ids < TILE * counts[part], slots[...], -1)


def mask_slots(counts, slots):
    return pl.pallas_call(
        mask_kernel,
        out_shape=shape(*slots.shape, dtype=i32),
        in_specs=[SMEM, VMEM],
        out_specs=VMEM,
        compiler_params=params(),
        name="mask_slots",
    )(counts, slots)


def gain_terms(gain, width):
    high = gain.astype(bf16)
    middle = (gain - high.astype(f32)).astype(bf16)
    low = (gain - high.astype(f32) - middle.astype(f32)).astype(bf16)
    row_ids = lax.broadcasted_iota(i32, (GAIN_ROWS, width), 0)
    rows = jnp.where(row_ids == 0, high.astype(f32), 0.0)
    rows = jnp.where(row_ids == 1, middle.astype(f32), rows)
    return jnp.where(row_ids == 2, low.astype(f32), rows).astype(bf16)


def block_kernel(ways, split, early, edges, gain, *rest):
    blocks, sems = rest[:-1], rest[-1]
    copy, finish = copier(sems)
    me = lax.axis_index("chan")
    width = edges.shape[1]
    for d in range(1, ways):
        row = pl.multiple_of(lax.rem(me + d, ways) * split, TILE)
        copy(edges.at[pl.ds(row, split), :], blocks[d - 1].at[pl.ds(0, split), :])
        if early:
            copy(edges.at[pl.ds(ways * split, early), :], blocks[d - 1].at[pl.ds(split, early), :])
        blocks[d - 1][split + early :, :] = gain_terms(gain[...], width)
    if len(blocks) == ways:
        late = blocks[-1].shape[0]
        copy(edges.at[pl.ds(ways * split + early, late), :], blocks[-1])
    finish()


def prepare_blocks(edge_feats, gain, ways, split, early, late):
    width = edge_feats.shape[1]
    outs = [shape(split + early + GAIN_ROWS, width)] * (ways - 1) + [shape(late, width)] * (late > 0)
    copies = (ways - 1) * (2 if early else 1) + (late > 0)
    return pl.pallas_call(
        functools.partial(block_kernel, ways, split, early),
        out_shape=outs,
        in_specs=[HBM, VMEM],
        out_specs=[VMEM] * len(outs),
        scratch_shapes=[pltpu.SemaphoreType.DMA((copies,))],
        compiler_params=params(),
        name="prepare_blocks",
    )(edge_feats, gain)


def halo_kernel(ways, rows_ref, *refs):
    nodes, halos = refs[:ways], refs[ways:]
    count, width = nodes[0].shape
    for j, halo in enumerate(halos):
        hits = onehot(column(rows_ref[0, j : j + 1, :]), count)
        for d in range(ways):
            halo[:, d * width : (d + 1) * width] = dot(hits, nodes[d][...]).astype(bf16)


def halo_gather(halo_rows, nodes):
    ways = len(nodes)
    _, offsets, size = halo_rows.shape
    return pl.pallas_call(
        functools.partial(halo_kernel, ways),
        out_shape=[shape(size, ways * nodes[0].shape[1])] * offsets,
        compiler_params=params(),
        cost_estimate=pl.CostEstimate(flops=6 * 10**9, bytes_accessed=4 * 1024 * 1024, transcendentals=0),
        name="halo_gather",
    )(halo_rows, *nodes)


def join_kernel(first, second, out):
    rows = first.shape[1]
    out[:, :rows, :] = first[...]
    out[:, rows:, :] = second[...]


def join(first, second):
    parts, rows, channels = first.shape
    return pl.pallas_call(
        join_kernel,
        out_shape=shape(parts, 2 * rows, channels),
        compiler_params=params(),
        name="join",
    )(first, second)


def gather_shares(piece, axes, waits):
    pieces = [piece]
    for axis in axes:
        if axis == "rep":
            pieces[-1] = tie(pieces[-1], *waits)
        pieces = pieces + [swapped(p, axis) for p in pieces]
    return pieces


def assemble_kernel(axes, *refs):
    pieces, out = refs[:-1], refs[-1]
    share = share_index(axes)
    each = (1 << len(axes)) // len(pieces)
    rows = pieces[0].shape[1] // each
    for m in range(len(pieces) * each):
        start = pl.multiple_of((share ^ m) * rows, rows)
        place = m % each * rows
        for part in range(out.shape[0]):
            out[part, pl.ds(start, rows), :] = pieces[m // each][part, place : place + rows, :]


def assemble(pieces, axes):
    parts, rows, channels = pieces[0].shape
    return pl.pallas_call(
        functools.partial(assemble_kernel, axes),
        out_shape=shape(parts, rows * len(pieces), channels),
        compiler_params=params(),
        name="assemble",
    )(*pieces)


def stage_kernel(w_in, w_out, inner, outer, sems):
    copy, finish = copier(sems)
    copy(w_in, inner)
    copy(w_out, outer)
    finish()


def stage(weight_in, weight_out):
    return pl.pallas_call(
        stage_kernel,
        out_shape=[shape(*weight_in.shape), shape(*weight_out.shape)],
        in_specs=[HBM] * 2,
        out_specs=[VMEM] * 2,
        scratch_shapes=[pltpu.SemaphoreType.DMA((2,))],
        compiler_params=params(),
        name="stage",
    )(weight_in, weight_out)


def plan_rows(slot_count, ways):
    tiles = slot_count // TILE
    shared = [2, 2] if ways == 2 and tiles >= 8 and tiles % 2 == 0 else []
    alone = (tiles - sum(shared)) // ways
    chunks = [alone - alone // 2, alone // 2]
    return [size * TILE for size in chunks if size], [size * TILE for size in shared]


def starts_of(sizes):
    return [sum(sizes[:k]) for k in range(len(sizes))]


def edge_kernel(ways, place, mine, late, sender_ref, slot_ref, *refs):
    refs = list(refs)

    def take(count):
        taken = refs[:count]
        del refs[:count]
        return taken

    (own, own_gain), mains, others = take(2), take(ways - 1), take(ways - 1 if late else 0)
    nodes, halos = take(ways), take(2 * RADIUS)
    w_in, w_out = take(2)
    others_a, others_b = take(ways - 1), take(ways - 1)
    outs = refs
    width = own.shape[1]
    channels = ways * width
    me = lax.axis_index("chan")
    split, base, start = place
    first = pl.multiple_of(me * split + base, TILE)
    edges = [own[pl.ds(first, mine), :]]
    for d, block in enumerate(mains):
        here = mine - others[d].shape[0] if late else mine
        rows = block[start : start + here, :]
        edges.append(jnp.concatenate([rows, others[d][...]], axis=0) if late else rows)
    local_nodes = nodes[0].shape[0]
    halo_count = sum(h.shape[0] for h in halos)
    to_sender = onehot(column(sender_ref[:, pl.ds(first, mine)]), local_nodes)
    slots = column(slot_ref[:, pl.ds(first, mine)])
    to_slot = onehot(slots, local_nodes + halo_count)
    table = jnp.concatenate([h[...] for h in halos], axis=0)
    preact = None
    for d in range(ways):
        if d == 0:
            weights = (w_in[0], w_in[1], w_in[2])
        else:
            weights = (others_a[d - 1][0], others_a[d - 1][1], others_b[d - 1][0])
        sent = dot(to_sender, nodes[d][...]).astype(bf16)
        got = dot(to_slot[:, :local_nodes], nodes[d][...])
        got = (got + dot(to_slot[:, local_nodes:], table[:, d * width : (d + 1) * width])).astype(bf16)
        term = dot(edges[d], weights[0]) + dot(sent, weights[1]) + dot(got, weights[2])
        preact = term if preact is None else preact + term
    hidden = (0.5 * preact * (1.0 + jnp.tanh(0.5 * preact))).astype(bf16)
    projected = [dot(hidden, w_out[...])]
    for d in range(1, ways):
        blocks = [slice(h * width, (h + 1) * width) for h in range(ways)]
        projected.append(sum(dot(hidden[:, b], others_b[d - 1][1, :, b]) for b in blocks))
    mean = sum(jnp.sum(p, axis=1, keepdims=True) for p in projected) / channels
    square = sum(jnp.sum(p * p, axis=1, keepdims=True) for p in projected) / channels
    scale = lax.rsqrt(square - mean * mean + 1e-05)
    live = jnp.concatenate([slots] * (width // 128), axis=1) >= 0
    for d in range(len(outs)):
        if d == 0:
            gain = own_gain[...]
        else:
            terms = mains[d - 1][mains[d - 1].shape[0] - GAIN_ROWS :, :].astype(f32)
            gain = terms[0:1, :] + terms[1:2, :] + terms[2:3, :]
        normed = (projected[d] - mean) * scale * gain
        outs[d][...] = jnp.where(live, (edges[d].astype(f32) + normed).astype(bf16), edges[d])


def edge_update(k, place, mine, results, senders, slots, own, gain, blocks, others, nodes, halos, w_in, w_out, others_a, others_b):
    ways = len(nodes)
    width = own.shape[1]
    channels = ways * width
    operands = [own, gain, *blocks, *others, *nodes, *halos, w_in, w_out, *others_a, *others_b]
    return pl.pallas_call(
        functools.partial(edge_kernel, ways, place, mine, bool(others)),
        out_shape=[shape(mine, width)] * results,
        in_specs=[VMEM] * (2 + len(operands)),
        out_specs=[VMEM] * results,
        compiler_params=params(),
        cost_estimate=pl.CostEstimate(
            flops=2 * mine * channels * (4 * channels + 768),
            bytes_accessed=8 * channels * channels,
            transcendentals=mine * channels,
        ),
        name=f"edge_update_{k}",
    )(senders, slots, *operands)


def collect_kernel(ways, places, local_nodes, last, slot_ref, *refs):
    refs = list(refs)
    parts = [refs.pop(0) for _ in places]
    sums = refs.pop(0)[...] if len(refs) > (1 + 2 * RADIUS if last else 1) else None
    me = lax.axis_index("chan")
    table_rows = refs[0].shape[0] + (sum(r.shape[0] for r in refs[1:]) if last else 0)
    for (d, split, base), block in zip(places, parts):
        mine = block.shape[0]
        first = pl.multiple_of(lax.rem(me + d, ways) * split + base, TILE)
        slots = slot_ref[:, pl.ds(first, mine)]
        rows = lax.broadcasted_iota(i32, (table_rows, mine), 0)
        hits = (rows == jnp.broadcast_to(slots, (table_rows, mine))).astype(f32).astype(bf16)
        term = dot(hits, block[...])
        sums = term if sums is None else sums + term
    if not last:
        refs[0][...] = sums
        return
    refs[0][...] = sums[:local_nodes]
    start = local_nodes
    for out in refs[1:]:
        size = out.shape[0]
        out[...] = sums[start : start + size].astype(bf16)
        start += size


def collect(places, parts, sums, slots, ways, local_nodes, halo_size, last):
    width = parts[0].shape[1]
    table_rows = local_nodes + 2 * RADIUS * halo_size
    before = [] if sums is None else [sums]
    if last:
        outs = [shape(local_nodes, width, dtype=f32)] + [shape(halo_size, width)] * (2 * RADIUS)
    else:
        outs = [shape(table_rows, width, dtype=f32)]
    return pl.pallas_call(
        functools.partial(collect_kernel, ways, places, local_nodes, last),
        out_shape=outs,
        in_specs=[VMEM] * (1 + len(parts) + len(before)),
        out_specs=[VMEM] * len(outs),
        compiler_params=params(),
        name="collect",
    )(slots, *parts, *before)


def write_kernel(ways, places, *refs):
    parts, out = refs[:-1], refs[-1]
    me = lax.axis_index("chan")
    for (d, split, base), block in zip(places, parts):
        first = pl.multiple_of(lax.rem(me + d, ways) * split + base, TILE)
        out[pl.ds(first, block.shape[0]), :] = block[...]


def write(places, parts, slot_count, ways):
    return pl.pallas_call(
        functools.partial(write_kernel, ways, places),
        out_shape=shape(slot_count, parts[0].shape[1]),
        compiler_params=params(),
        name="write",
    )(*parts)


def finish_kernel(rows_ref, own, *refs):
    returned, out = refs[:-1], refs[-1]
    hits = []
    for j, rows in enumerate(returned):
        ids = lax.broadcasted_iota(i32, (own.shape[0], rows.shape[0]), 0)
        hits.append((ids == jnp.broadcast_to(rows_ref[0, j : j + 1, :], ids.shape)).astype(f32).astype(bf16))
    rows = jnp.concatenate([r[...] for r in returned], axis=0)
    out[...] = own[...] + dot(jnp.concatenate(hits, axis=1), rows)


def finish(halo_rows, own, returned):
    return pl.pallas_call(
        finish_kernel,
        out_shape=shape(*own.shape, dtype=f32),
        compiler_params=params(),
        name="finish",
    )(halo_rows, own, *returned)


def local(
    node_feats,
    edge_feats,
    senders,
    receiver_slot,
    halo_rows,
    tile_counts,
    weight_in,
    weight_out,
    norm_gain,
):
    ways = lax.axis_size("chan")
    offsets = [shift_by for shift_by in range(-RADIUS, RADIUS + 1) if shift_by != 0]
    local_nodes, width = node_feats.shape
    halo_size = halo_rows.shape[2]
    slot_count = edge_feats.shape[0]
    alone, shared = plan_rows(slot_count, ways)
    split, early, late = sum(alone), sum(shared[:1]), sum(shared[1:])
    distances = range(1, ways)
    axes_a, axes_b = even(SHARERS_A), even(SHARERS_B)

    gain = norm_gain.reshape(1, width)
    sender_row, slot_row = senders.reshape(1, -1), mask_slots(tile_counts, receiver_slot.reshape(1, -1))
    message_a = prepare_first(weight_in, axes_a)
    message_b = prepare_second(weight_in, weight_out, ways, axes_b)
    blocks = prepare_blocks(edge_feats, gain, ways, split, early, late)
    blocks = [tie(block, sender_row, slot_row) for block in blocks]
    nodes = [node_feats] + [shifted(node_feats, "chan", d) for d in distances]
    crossed_a = [shifted(message_a, "chan", d) for d in distances]
    crossed_b = [shifted(message_b, "chan", d) for d in distances]
    outgoing = halo_gather(halo_rows, nodes)
    halos = [shifted(rows, ("dom", "rep"), by) for rows, by in zip(outgoing, offsets)]
    edges = [shifted(blocks[d - 1], "chan", d) for d in distances]
    late_edges = [shifted(blocks[-1], "chan", d) for d in distances if late]
    pieces = [tie(piece, *halos[:3]) for piece in crossed_a]
    pieces = [join(piece, swapped(piece, axes_a[0])) for piece in pieces]
    pieces = [tie(piece, *halos[3:]) for piece in pieces]
    crossed_b = [tie(piece, *pieces) for piece in crossed_b]
    others_a = [assemble(gather_shares(piece, axes_a[1:], edges), axes_a) for piece in pieces]
    inner, outer = stage(tie(weight_in, *outgoing), weight_out)
    others_b = [assemble(gather_shares(piece, axes_b, [inner, outer]), axes_b) for piece in crossed_b]

    def collected(places, parts, sums, last=False):
        return collect(places, parts, sums, slot_row, ways, local_nodes, halo_size, last)

    jobs = [(split, before, before, mine, ways) for before, mine in zip(starts_of(alone), alone)]
    if shared:
        jobs.append((0, ways * split, split, early + late, 1))
    parts, places, order = [], [], edge_feats
    for k, (stride, base, start, mine, results) in enumerate(jobs):
        others = late_edges if k == len(alone) else []
        outs = edge_update(
            k, (stride, base, start), mine, results, sender_row, slot_row, order, gain, edges, others,
            nodes, halos, inner, outer, others_a, others_b,
        )
        order = tie(order, *outs)
        outs = [outs[0]] + [shifted(outs[d], "chan", -d) for d in range(1, results)]
        parts.append(outs)
        places.append([(d, stride, base) for d in range(results)])

    def chosen(which):
        return [places[k][d] for k, d in which], [parts[k][d] for k, d in which]

    count = len(alone)
    final = [(count - 1, d) for d in distances]
    own_parts = [(k, 0) for k in range(len(jobs))]
    (sums,) = collected(*chosen(own_parts + [(k, d) for k in range(count - 1) for d in distances]), None)
    own, *pieces = collected(*chosen(final), sums, True)
    returned = [shifted(piece, ("dom", "rep"), -by) for piece, by in zip(pieces, offsets)]
    everything = chosen([(k, d) for k, outs in enumerate(parts) for d in range(len(outs))])
    return (write(*everything, slot_count, ways), finish(halo_rows, own, returned))


def solution(mesh):
    placed = (
        P(("groups", "dom", "rep"), "chan"),
        P(("groups", "dom", "rep"), "chan"),
        P(("groups", "dom", "rep")),
        P(("groups", "dom", "rep")),
        P(("groups", "dom", "rep"), None, None),
        P("groups"),
        P(None, "chan", None),
        P(None, "chan"),
        P("chan"),
    )
    return jax.shard_map(
        local,
        mesh=mesh,
        in_specs=placed,
        out_specs=(P(("groups", "dom", "rep"), "chan"), P(("groups", "dom", "rep"), "chan")),
        check_vma=False,
    )
```

```python
import functools

import jax
import jax.numpy as jnp
from jax import lax
from jax.experimental import pallas as pl
from jax.experimental.pallas import tpu as pltpu
from jax.sharding import PartitionSpec as P

TILE = 128
RADIUS = 2
GAIN_ROWS = 16
SHARERS_A = ("groups", "dom", "rep")
SHARERS_B = ("groups", "rep")
bf16 = jnp.bfloat16
f32 = jnp.float32
i32 = jnp.int32
VMEM_BYTES = 24 * 1024 * 1024
PREPARE_VMEM_BYTES = 60 * 1024 * 1024
HBM = pl.BlockSpec(memory_space=pltpu.HBM)
VMEM = pl.BlockSpec(memory_space=pltpu.VMEM)
SMEM = pl.BlockSpec(memory_space=pltpu.SMEM)


def shape(*dims, dtype=bf16):
    return jax.ShapeDtypeStruct(dims, dtype)


def params(vmem=VMEM_BYTES):
    return pltpu.CompilerParams(vmem_limit_bytes=vmem)


def shifted(block, axis, distance):
    size = lax.axis_size(axis)
    return lax.ppermute(block, axis, [(i, (i + distance) % size) for i in range(size)])


def swapped(block, axis):
    size = lax.axis_size(axis)
    return lax.ppermute(block, axis, [(i, i ^ 1) for i in range(size)])


def even(axes):
    return [axis for axis in axes if lax.axis_size(axis) % 2 == 0]


def share_index(axes):
    return sum((lax.axis_index(axis) % 2) << place for place, axis in enumerate(axes))


def tie(array, *others):
    return lax.optimization_barrier((array, *others))[0]


def dot(a, b):
    return jnp.dot(a, b, preferred_element_type=f32)


def column(row):
    return jnp.transpose(jnp.broadcast_to(row, (128, row.shape[1])))


def onehot(ids, count):
    lanes = lax.broadcasted_iota(i32, ids.shape, 1)
    hits = [(ids == lanes + base).astype(f32).astype(bf16) for base in range(0, count, 128)]
    return jnp.concatenate(hits, axis=1) if len(hits) > 1 else hits[0]


def copier(sems):
    copies = []

    def copy(source, target):
        copies.append(pltpu.make_async_copy(source, target, sems.at[len(copies)]))
        copies[-1].start()

    def finish():
        for c in copies:
            c.wait()

    return copy, finish


def first_kernel(axes, w_in, first, sems):
    copy, finish = copier(sems)
    rows = w_in.shape[1] >> len(axes)
    start = pl.multiple_of(share_index(axes) * rows, rows)
    for part in range(2):
        copy(w_in.at[part, pl.ds(start, rows), :], first.at[part])
    finish()


def prepare_first(weight_in, axes):
    _, width, channels = weight_in.shape
    return pl.pallas_call(
        functools.partial(first_kernel, axes),
        out_shape=shape(2, width >> len(axes), channels),
        in_specs=[HBM],
        out_specs=VMEM,
        scratch_shapes=[pltpu.SemaphoreType.DMA((2,))],
        compiler_params=params(PREPARE_VMEM_BYTES),
        name="prepare_first",
    )(weight_in)


def second_kernel(ways, axes, w_in, w_out, second, sems):
    copy, finish = copier(sems)
    width = w_out.shape[1]
    rows = width >> len(axes)
    start = pl.multiple_of(share_index(axes) * rows, rows)
    copy(w_in.at[2, pl.ds(start, rows), :], second.at[0])
    for h in range(ways):
        copy(w_out.at[pl.ds(h * width + start, rows), :], second.at[1, :, pl.ds(h * width, width)])
    finish()


def prepare_second(weight_in, weight_out, ways, axes):
    width = weight_out.shape[1]
    return pl.pallas_call(
        functools.partial(second_kernel, ways, axes),
        out_shape=shape(2, width >> len(axes), ways * width),
        in_specs=[HBM, HBM],
        out_specs=VMEM,
        scratch_shapes=[pltpu.SemaphoreType.DMA((1 + ways,))],
        compiler_params=params(PREPARE_VMEM_BYTES),
        name="prepare_second",
    )(weight_in, weight_out)


def mask_kernel(counts, slots, out):
    part = lax.axis_index("dom") * lax.axis_size("rep") + lax.axis_index("rep")
    ids = lax.broadcasted_iota(i32, slots.shape, 1)
    out[...] = jnp.where(ids < TILE * counts[part], slots[...], -1)


def mask_slots(counts, slots):
    return pl.pallas_call(
        mask_kernel,
        out_shape=shape(*slots.shape, dtype=i32),
        in_specs=[SMEM, VMEM],
        out_specs=VMEM,
        compiler_params=params(),
        name="mask_slots",
    )(counts, slots)


def gain_terms(gain, width):
    high = gain.astype(bf16)
    middle = (gain - high.astype(f32)).astype(bf16)
    low = (gain - high.astype(f32) - middle.astype(f32)).astype(bf16)
    row_ids = lax.broadcasted_iota(i32, (GAIN_ROWS, width), 0)
    rows = jnp.where(row_ids == 0, high.astype(f32), 0.0)
    rows = jnp.where(row_ids == 1, middle.astype(f32), rows)
    return jnp.where(row_ids == 2, low.astype(f32), rows).astype(bf16)


def block_kernel(ways, split, early, edges, gain, *rest):
    blocks, sems = rest[:-1], rest[-1]
    copy, finish = copier(sems)
    me = lax.axis_index("chan")
    width = edges.shape[1]
    for d in range(1, ways):
        row = pl.multiple_of(lax.rem(me + d, ways) * split, TILE)
        copy(edges.at[pl.ds(row, split), :], blocks[d - 1].at[pl.ds(0, split), :])
        if early:
            copy(edges.at[pl.ds(ways * split, early), :], blocks[d - 1].at[pl.ds(split, early), :])
        blocks[d - 1][split + early :, :] = gain_terms(gain[...], width)
    if len(blocks) == ways:
        late = blocks[-1].shape[0]
        copy(edges.at[pl.ds(ways * split + early, late), :], blocks[-1])
    finish()


def prepare_blocks(edge_feats, gain, ways, split, early, late):
    width = edge_feats.shape[1]
    outs = [shape(split + early + GAIN_ROWS, width)] * (ways - 1) + [shape(late, width)] * (late > 0)
    copies = (ways - 1) * (2 if early else 1) + (late > 0)
    return pl.pallas_call(
        functools.partial(block_kernel, ways, split, early),
        out_shape=outs,
        in_specs=[HBM, VMEM],
        out_specs=[VMEM] * len(outs),
        scratch_shapes=[pltpu.SemaphoreType.DMA((copies,))],
        compiler_params=params(),
        name="prepare_blocks",
    )(edge_feats, gain)


def halo_kernel(ways, rows_ref, *refs):
    nodes, halos = refs[:ways], refs[ways:]
    count, width = nodes[0].shape
    for j, halo in enumerate(halos):
        hits = onehot(column(rows_ref[0, j : j + 1, :]), count)
        for d in range(ways):
            halo[:, d * width : (d + 1) * width] = dot(hits, nodes[d][...]).astype(bf16)


def halo_gather(halo_rows, nodes):
    ways = len(nodes)
    _, offsets, size = halo_rows.shape
    return pl.pallas_call(
        functools.partial(halo_kernel, ways),
        out_shape=[shape(size, ways * nodes[0].shape[1])] * offsets,
        compiler_params=params(),
        cost_estimate=pl.CostEstimate(flops=6 * 10**9, bytes_accessed=4 * 1024 * 1024, transcendentals=0),
        name="halo_gather",
    )(halo_rows, *nodes)


def join_kernel(first, second, out):
    rows = first.shape[1]
    out[:, :rows, :] = first[...]
    out[:, rows:, :] = second[...]


def join(first, second):
    parts, rows, channels = first.shape
    return pl.pallas_call(
        join_kernel,
        out_shape=shape(parts, 2 * rows, channels),
        compiler_params=params(),
        name="join",
    )(first, second)


def gather_shares(piece, axes, waits):
    pieces = [piece]
    for axis in axes:
        if axis == "rep":
            pieces[-1] = tie(pieces[-1], *waits)
        pieces = pieces + [swapped(p, axis) for p in pieces]
    return pieces


def assemble_part(axes, pieces, out):
    share = share_index(axes)
    each = (1 << len(axes)) // len(pieces)
    rows = pieces[0].shape[1] // each
    for m in range(len(pieces) * each):
        start = pl.multiple_of((share ^ m) * rows, rows)
        place = m % each * rows
        for part in range(out.shape[0]):
            out[part, pl.ds(start, rows), :] = pieces[m // each][part, place : place + rows, :]


def assemble_kernel(groups, *refs):
    sources, outs = refs[: -len(groups)], refs[-len(groups) :]
    for (axes, count), out in zip(groups, outs):
        assemble_part(axes, sources[:count], out)
        sources = sources[count:]


def assemble(groups):
    parts, rows, channels = groups[0][0][0].shape
    return pl.pallas_call(
        functools.partial(assemble_kernel, [(axes, len(pieces)) for pieces, axes in groups]),
        out_shape=[shape(pieces[0].shape[0], pieces[0].shape[1] * len(pieces), channels) for pieces, _ in groups],
        compiler_params=params(),
        name="assemble",
    )(*[piece for pieces, _ in groups for piece in pieces])


def stage_kernel(w_in, w_out, inner, outer, sems):
    copy, finish = copier(sems)
    copy(w_in, inner)
    copy(w_out, outer)
    finish()


def stage(weight_in, weight_out):
    return pl.pallas_call(
        stage_kernel,
        out_shape=[shape(*weight_in.shape), shape(*weight_out.shape)],
        in_specs=[HBM] * 2,
        out_specs=[VMEM] * 2,
        scratch_shapes=[pltpu.SemaphoreType.DMA((2,))],
        compiler_params=params(),
        name="stage",
    )(weight_in, weight_out)


def plan_rows(slot_count, ways):
    tiles = slot_count // TILE
    shared = [2, 2] if ways == 2 and tiles >= 8 and tiles % 2 == 0 else []
    alone = (tiles - sum(shared)) // ways
    chunks = [alone - alone // 2, alone // 2]
    return [size * TILE for size in chunks if size], [size * TILE for size in shared]


def starts_of(sizes):
    return [sum(sizes[:k]) for k in range(len(sizes))]


def edge_kernel(ways, place, mine, late, sender_ref, slot_ref, *refs):
    refs = list(refs)

    def take(count):
        taken = refs[:count]
        del refs[:count]
        return taken

    (own, own_gain), mains, others = take(2), take(ways - 1), take(ways - 1 if late else 0)
    nodes, halos = take(ways), take(2 * RADIUS)
    w_in, w_out = take(2)
    others_a, others_b = take(ways - 1), take(ways - 1)
    outs = refs
    width = own.shape[1]
    channels = ways * width
    me = lax.axis_index("chan")
    split, base, start = place
    first = pl.multiple_of(me * split + base, TILE)
    edges = [own[pl.ds(first, mine), :]]
    for d, block in enumerate(mains):
        here = mine - others[d].shape[0] if late else mine
        rows = block[start : start + here, :]
        edges.append(jnp.concatenate([rows, others[d][...]], axis=0) if late else rows)
    local_nodes = nodes[0].shape[0]
    halo_count = sum(h.shape[0] for h in halos)
    to_sender = onehot(column(sender_ref[:, pl.ds(first, mine)]), local_nodes)
    slots = column(slot_ref[:, pl.ds(first, mine)])
    to_slot = onehot(slots, local_nodes + halo_count)
    table = jnp.concatenate([h[...] for h in halos], axis=0)
    preact = None
    for d in range(ways):
        if d == 0:
            weights = (w_in[0], w_in[1], w_in[2])
        else:
            weights = (others_a[d - 1][0], others_a[d - 1][1], others_b[d - 1][0])
        sent = dot(to_sender, nodes[d][...]).astype(bf16)
        got = dot(to_slot[:, :local_nodes], nodes[d][...])
        got = (got + dot(to_slot[:, local_nodes:], table[:, d * width : (d + 1) * width])).astype(bf16)
        term = dot(edges[d], weights[0]) + dot(sent, weights[1]) + dot(got, weights[2])
        preact = term if preact is None else preact + term
    hidden = (0.5 * preact * (1.0 + jnp.tanh(0.5 * preact))).astype(bf16)
    projected = [dot(hidden, w_out[...])]
    for d in range(1, ways):
        blocks = [slice(h * width, (h + 1) * width) for h in range(ways)]
        projected.append(sum(dot(hidden[:, b], others_b[d - 1][1, :, b]) for b in blocks))
    mean = sum(jnp.sum(p, axis=1, keepdims=True) for p in projected) / channels
    square = sum(jnp.sum(p * p, axis=1, keepdims=True) for p in projected) / channels
    scale = lax.rsqrt(square - mean * mean + 1e-05)
    live = jnp.concatenate([slots] * (width // 128), axis=1) >= 0
    for d in range(len(outs)):
        if d == 0:
            gain = own_gain[...]
        else:
            terms = mains[d - 1][mains[d - 1].shape[0] - GAIN_ROWS :, :].astype(f32)
            gain = terms[0:1, :] + terms[1:2, :] + terms[2:3, :]
        normed = (projected[d] - mean) * scale * gain
        outs[d][...] = jnp.where(live, (edges[d].astype(f32) + normed).astype(bf16), edges[d])


def edge_update(k, place, mine, results, senders, slots, own, gain, blocks, others, nodes, halos, w_in, w_out, others_a, others_b):
    ways = len(nodes)
    width = own.shape[1]
    channels = ways * width
    operands = [own, gain, *blocks, *others, *nodes, *halos, w_in, w_out, *others_a, *others_b]
    return pl.pallas_call(
        functools.partial(edge_kernel, ways, place, mine, bool(others)),
        out_shape=[shape(mine, width)] * results,
        in_specs=[VMEM] * (2 + len(operands)),
        out_specs=[VMEM] * results,
        compiler_params=params(),
        cost_estimate=pl.CostEstimate(
            flops=2 * mine * channels * (4 * channels + 768),
            bytes_accessed=8 * channels * channels,
            transcendentals=mine * channels,
        ),
        name=f"edge_update_{k}",
    )(senders, slots, *operands)


def collect_kernel(ways, places, local_nodes, last, slot_ref, *refs):
    refs = list(refs)
    parts = [refs.pop(0) for _ in places]
    sums = refs.pop(0)[...] if len(refs) > (1 + 2 * RADIUS if last else 1) else None
    me = lax.axis_index("chan")
    table_rows = refs[0].shape[0] + (sum(r.shape[0] for r in refs[1:]) if last else 0)
    for (d, split, base), block in zip(places, parts):
        mine = block.shape[0]
        first = pl.multiple_of(lax.rem(me + d, ways) * split + base, TILE)
        slots = slot_ref[:, pl.ds(first, mine)]
        rows = lax.broadcasted_iota(i32, (table_rows, mine), 0)
        hits = (rows == jnp.broadcast_to(slots, (table_rows, mine))).astype(f32).astype(bf16)
        term = dot(hits, block[...])
        sums = term if sums is None else sums + term
    if not last:
        refs[0][...] = sums
        return
    refs[0][...] = sums[:local_nodes]
    start = local_nodes
    for out in refs[1:]:
        size = out.shape[0]
        out[...] = sums[start : start + size].astype(bf16)
        start += size


def collect(places, parts, sums, slots, ways, local_nodes, halo_size, last):
    width = parts[0].shape[1]
    table_rows = local_nodes + 2 * RADIUS * halo_size
    before = [] if sums is None else [sums]
    if last:
        outs = [shape(local_nodes, width, dtype=f32)] + [shape(halo_size, width)] * (2 * RADIUS)
    else:
        outs = [shape(table_rows, width, dtype=f32)]
    return pl.pallas_call(
        functools.partial(collect_kernel, ways, places, local_nodes, last),
        out_shape=outs,
        in_specs=[VMEM] * (1 + len(parts) + len(before)),
        out_specs=[VMEM] * len(outs),
        compiler_params=params(),
        name="collect",
    )(slots, *parts, *before)


def write_kernel(ways, places, *refs):
    parts, out = refs[:-1], refs[-1]
    me = lax.axis_index("chan")
    for (d, split, base), block in zip(places, parts):
        first = pl.multiple_of(lax.rem(me + d, ways) * split + base, TILE)
        out[pl.ds(first, block.shape[0]), :] = block[...]


def write(places, parts, slot_count, ways):
    return pl.pallas_call(
        functools.partial(write_kernel, ways, places),
        out_shape=shape(slot_count, parts[0].shape[1]),
        compiler_params=params(),
        name="write",
    )(*parts)


def finish_kernel(rows_ref, own, *refs):
    returned, out = refs[:-1], refs[-1]
    hits = []
    for j, rows in enumerate(returned):
        ids = lax.broadcasted_iota(i32, (own.shape[0], rows.shape[0]), 0)
        hits.append((ids == jnp.broadcast_to(rows_ref[0, j : j + 1, :], ids.shape)).astype(f32).astype(bf16))
    rows = jnp.concatenate([r[...] for r in returned], axis=0)
    out[...] = own[...] + dot(jnp.concatenate(hits, axis=1), rows)


def finish(halo_rows, own, returned):
    return pl.pallas_call(
        finish_kernel,
        out_shape=shape(*own.shape, dtype=f32),
        compiler_params=params(),
        name="finish",
    )(halo_rows, own, *returned)


def local(
    node_feats,
    edge_feats,
    senders,
    receiver_slot,
    halo_rows,
    tile_counts,
    weight_in,
    weight_out,
    norm_gain,
):
    ways = lax.axis_size("chan")
    offsets = [shift_by for shift_by in range(-RADIUS, RADIUS + 1) if shift_by != 0]
    local_nodes, width = node_feats.shape
    halo_size = halo_rows.shape[2]
    slot_count = edge_feats.shape[0]
    alone, shared = plan_rows(slot_count, ways)
    split, early, late = sum(alone), sum(shared[:1]), sum(shared[1:])
    distances = range(1, ways)
    axes_a, axes_b = even(SHARERS_A), even(SHARERS_B)

    gain = norm_gain.reshape(1, width)
    sender_row, slot_row = senders.reshape(1, -1), mask_slots(tile_counts, receiver_slot.reshape(1, -1))
    message_a = prepare_first(weight_in, axes_a)
    message_b = prepare_second(weight_in, weight_out, ways, axes_b)
    blocks = prepare_blocks(edge_feats, gain, ways, split, early, late)
    blocks = [tie(block, sender_row, slot_row) for block in blocks]
    nodes = [node_feats] + [shifted(node_feats, "chan", d) for d in distances]
    crossed_a = [shifted(message_a, "chan", d) for d in distances]
    crossed_b = [shifted(message_b, "chan", d) for d in distances]
    outgoing = halo_gather(halo_rows, nodes)
    halos = [shifted(rows, ("dom", "rep"), by) for rows, by in zip(outgoing, offsets)]
    edges = [shifted(blocks[d - 1], "chan", d) for d in distances]
    late_edges = [shifted(blocks[-1], "chan", d) for d in distances if late]
    pieces = [tie(piece, *halos[:3]) for piece in crossed_a]
    pieces = [join(piece, swapped(piece, axes_a[0])) for piece in pieces]
    pieces = [tie(piece, *halos[3:]) for piece in pieces]
    crossed_b = [tie(piece, *pieces) for piece in crossed_b]
    groups_a = [(gather_shares(piece, axes_a[1:], []), axes_a) for piece in pieces]
    inner, outer = stage(tie(weight_in, *outgoing), weight_out)
    groups_b = [(gather_shares(piece, axes_b, [inner, outer, *edges]), axes_b) for piece in crossed_b]
    others = assemble(groups_a + groups_b)
    others_a, others_b = others[: len(groups_a)], others[len(groups_a) :]

    def collected(places, parts, sums, last=False):
        return collect(places, parts, sums, slot_row, ways, local_nodes, halo_size, last)

    jobs = [(split, before, before, mine, ways) for before, mine in zip(starts_of(alone), alone)]
    if shared:
        jobs.append((0, ways * split, split, early + late, 1))
    parts, places, order = [], [], edge_feats
    for k, (stride, base, start, mine, results) in enumerate(jobs):
        late_rows = late_edges if k == len(alone) else []
        outs = edge_update(
            k, (stride, base, start), mine, results, sender_row, slot_row, order, gain, edges, late_rows,
            nodes, halos, inner, outer, others_a, others_b,
        )
        order = tie(order, *outs)
        outs = [outs[0]] + [shifted(outs[d], "chan", -d) for d in range(1, results)]
        parts.append(outs)
        places.append([(d, stride, base) for d in range(results)])

    def chosen(which):
        return [places[k][d] for k, d in which], [parts[k][d] for k, d in which]

    count = len(alone)
    final = [(count - 1, d) for d in distances]
    own_parts = [(k, 0) for k in range(len(jobs))]
    (sums,) = collected(*chosen(own_parts + [(k, d) for k in range(count - 1) for d in distances]), None)
    own, *pieces = collected(*chosen(final), sums, True)
    returned = [shifted(piece, ("dom", "rep"), -by) for piece, by in zip(pieces, offsets)]
    everything = chosen([(k, d) for k, outs in enumerate(parts) for d in range(len(outs))])
    return (write(*everything, slot_count, ways), finish(halo_rows, own, returned))


def solution(mesh):
    placed = (
        P(("groups", "dom", "rep"), "chan"),
        P(("groups", "dom", "rep"), "chan"),
        P(("groups", "dom", "rep")),
        P(("groups", "dom", "rep")),
        P(("groups", "dom", "rep"), None, None),
        P("groups"),
        P(None, "chan", None),
        P(None, "chan"),
        P("chan"),
    )
    return jax.shard_map(
        local,
        mesh=mesh,
        in_specs=placed,
        out_specs=(P(("groups", "dom", "rep"), "chan"), P(("groups", "dom", "rep"), "chan")),
        check_vma=False,
    )
```

```python
import functools

import jax
import jax.numpy as jnp
from jax import lax
from jax.experimental import pallas as pl
from jax.experimental.pallas import tpu as pltpu
from jax.sharding import PartitionSpec as P

TILE = 128
RADIUS = 2
GAIN_ROWS = 16
SHARERS_A = ("groups", "dom", "rep")
SHARERS_B = ("groups", "rep")
bf16 = jnp.bfloat16
f32 = jnp.float32
i32 = jnp.int32
VMEM_BYTES = 24 * 1024 * 1024
PREPARE_VMEM_BYTES = 60 * 1024 * 1024
HBM = pl.BlockSpec(memory_space=pltpu.HBM)
VMEM = pl.BlockSpec(memory_space=pltpu.VMEM)
SMEM = pl.BlockSpec(memory_space=pltpu.SMEM)


def shape(*dims, dtype=bf16):
    return jax.ShapeDtypeStruct(dims, dtype)


def params(vmem=VMEM_BYTES):
    return pltpu.CompilerParams(vmem_limit_bytes=vmem)


def shifted(block, axis, distance):
    size = lax.axis_size(axis)
    return lax.ppermute(block, axis, [(i, (i + distance) % size) for i in range(size)])


def swapped(block, axis):
    size = lax.axis_size(axis)
    return lax.ppermute(block, axis, [(i, i ^ 1) for i in range(size)])


def even(axes):
    return [axis for axis in axes if lax.axis_size(axis) % 2 == 0]


def share_index(axes):
    return sum((lax.axis_index(axis) % 2) << place for place, axis in enumerate(axes))


def tie(array, *others):
    return lax.optimization_barrier((array, *others))[0]


def dot(a, b):
    return jnp.dot(a, b, preferred_element_type=f32)


def column(row):
    return jnp.transpose(jnp.broadcast_to(row, (128, row.shape[1])))


def onehot(ids, count):
    lanes = lax.broadcasted_iota(i32, ids.shape, 1)
    hits = [(ids == lanes + base).astype(f32).astype(bf16) for base in range(0, count, 128)]
    return jnp.concatenate(hits, axis=1) if len(hits) > 1 else hits[0]


def copier(sems):
    copies = []

    def copy(source, target):
        copies.append(pltpu.make_async_copy(source, target, sems.at[len(copies)]))
        copies[-1].start()

    def finish():
        for c in copies:
            c.wait()

    return copy, finish


def first_kernel(axes, w_in, first, sems):
    copy, finish = copier(sems)
    rows = w_in.shape[1] >> len(axes)
    start = pl.multiple_of(share_index(axes) * rows, rows)
    for part in range(2):
        copy(w_in.at[part, pl.ds(start, rows), :], first.at[part])
    finish()


def prepare_first(weight_in, axes):
    _, width, channels = weight_in.shape
    return pl.pallas_call(
        functools.partial(first_kernel, axes),
        out_shape=shape(2, width >> len(axes), channels),
        in_specs=[HBM],
        out_specs=VMEM,
        scratch_shapes=[pltpu.SemaphoreType.DMA((2,))],
        compiler_params=params(PREPARE_VMEM_BYTES),
        name="prepare_first",
    )(weight_in)


def second_kernel(ways, axes, w_in, w_out, second, sems):
    copy, finish = copier(sems)
    width = w_out.shape[1]
    rows = width >> len(axes)
    start = pl.multiple_of(share_index(axes) * rows, rows)
    copy(w_in.at[2, pl.ds(start, rows), :], second.at[0])
    for h in range(ways):
        copy(w_out.at[pl.ds(h * width + start, rows), :], second.at[1, :, pl.ds(h * width, width)])
    finish()


def prepare_second(weight_in, weight_out, ways, axes):
    width = weight_out.shape[1]
    return pl.pallas_call(
        functools.partial(second_kernel, ways, axes),
        out_shape=shape(2, width >> len(axes), ways * width),
        in_specs=[HBM, HBM],
        out_specs=VMEM,
        scratch_shapes=[pltpu.SemaphoreType.DMA((1 + ways,))],
        compiler_params=params(PREPARE_VMEM_BYTES),
        name="prepare_second",
    )(weight_in, weight_out)


def mask_kernel(counts, slots, out):
    part = lax.axis_index("dom") * lax.axis_size("rep") + lax.axis_index("rep")
    ids = lax.broadcasted_iota(i32, slots.shape, 1)
    out[...] = jnp.where(ids < TILE * counts[part], slots[...], -1)


def mask_slots(counts, slots):
    return pl.pallas_call(
        mask_kernel,
        out_shape=shape(*slots.shape, dtype=i32),
        in_specs=[SMEM, VMEM],
        out_specs=VMEM,
        compiler_params=params(),
        name="mask_slots",
    )(counts, slots)


def gain_terms(gain, width):
    high = gain.astype(bf16)
    middle = (gain - high.astype(f32)).astype(bf16)
    low = (gain - high.astype(f32) - middle.astype(f32)).astype(bf16)
    row_ids = lax.broadcasted_iota(i32, (GAIN_ROWS, width), 0)
    rows = jnp.where(row_ids == 0, high.astype(f32), 0.0)
    rows = jnp.where(row_ids == 1, middle.astype(f32), rows)
    return jnp.where(row_ids == 2, low.astype(f32), rows).astype(bf16)


def block_kernel(ways, split, early, edges, gain, *rest):
    blocks, sems = rest[:-1], rest[-1]
    copy, finish = copier(sems)
    me = lax.axis_index("chan")
    width = edges.shape[1]
    for d in range(1, ways):
        row = pl.multiple_of(lax.rem(me + d, ways) * split, TILE)
        copy(edges.at[pl.ds(row, split), :], blocks[d - 1].at[pl.ds(0, split), :])
        if early:
            copy(edges.at[pl.ds(ways * split, early), :], blocks[d - 1].at[pl.ds(split, early), :])
        blocks[d - 1][split + early :, :] = gain_terms(gain[...], width)
    if len(blocks) == ways:
        late = blocks[-1].shape[0]
        copy(edges.at[pl.ds(ways * split + early, late), :], blocks[-1])
    finish()


def prepare_blocks(edge_feats, gain, ways, split, early, late):
    width = edge_feats.shape[1]
    outs = [shape(split + early + GAIN_ROWS, width)] * (ways - 1) + [shape(late, width)] * (late > 0)
    copies = (ways - 1) * (2 if early else 1) + (late > 0)
    return pl.pallas_call(
        functools.partial(block_kernel, ways, split, early),
        out_shape=outs,
        in_specs=[HBM, VMEM],
        out_specs=[VMEM] * len(outs),
        scratch_shapes=[pltpu.SemaphoreType.DMA((copies,))],
        compiler_params=params(),
        name="prepare_blocks",
    )(edge_feats, gain)


def halo_kernel(ways, rows_ref, *refs):
    nodes, halos = refs[:ways], refs[ways:]
    count, width = nodes[0].shape
    for j, halo in enumerate(halos):
        hits = onehot(column(rows_ref[0, j : j + 1, :]), count)
        for d in range(ways):
            halo[:, d * width : (d + 1) * width] = dot(hits, nodes[d][...]).astype(bf16)


def halo_gather(halo_rows, nodes):
    ways = len(nodes)
    _, offsets, size = halo_rows.shape
    return pl.pallas_call(
        functools.partial(halo_kernel, ways),
        out_shape=[shape(size, ways * nodes[0].shape[1])] * offsets,
        compiler_params=params(),
        cost_estimate=pl.CostEstimate(flops=6 * 10**9, bytes_accessed=4 * 1024 * 1024, transcendentals=0),
        name="halo_gather",
    )(halo_rows, *nodes)


def join_kernel(first, second, out):
    rows = first.shape[1]
    out[:, :rows, :] = first[...]
    out[:, rows:, :] = second[...]


def join(first, second):
    parts, rows, channels = first.shape
    return pl.pallas_call(
        join_kernel,
        out_shape=shape(parts, 2 * rows, channels),
        compiler_params=params(),
        name="join",
    )(first, second)


def gather_shares(piece, axes, waits):
    pieces = [piece]
    for axis in axes:
        if axis == "rep":
            pieces[-1] = tie(pieces[-1], *waits)
        pieces = pieces + [swapped(p, axis) for p in pieces]
    return pieces


def assemble_part(axes, pieces, out):
    share = share_index(axes)
    each = (1 << len(axes)) // len(pieces)
    rows = pieces[0].shape[1] // each
    for m in range(len(pieces) * each):
        start = pl.multiple_of((share ^ m) * rows, rows)
        place = m % each * rows
        for part in range(out.shape[0]):
            out[part, pl.ds(start, rows), :] = pieces[m // each][part, place : place + rows, :]


def assemble_kernel(groups, *refs):
    sources, outs = refs[: -len(groups)], refs[-len(groups) :]
    for (axes, count), out in zip(groups, outs):
        assemble_part(axes, sources[:count], out)
        sources = sources[count:]


def assemble(groups):
    parts, rows, channels = groups[0][0][0].shape
    return pl.pallas_call(
        functools.partial(assemble_kernel, [(axes, len(pieces)) for pieces, axes in groups]),
        out_shape=[shape(pieces[0].shape[0], pieces[0].shape[1] * len(pieces), channels) for pieces, _ in groups],
        compiler_params=params(),
        name="assemble",
    )(*[piece for pieces, _ in groups for piece in pieces])


def stage_kernel(w_in, w_out, inner, outer, sems):
    copy, finish = copier(sems)
    copy(w_in, inner)
    copy(w_out, outer)
    finish()


def stage(weight_in, weight_out):
    return pl.pallas_call(
        stage_kernel,
        out_shape=[shape(*weight_in.shape), shape(*weight_out.shape)],
        in_specs=[HBM] * 2,
        out_specs=[VMEM] * 2,
        scratch_shapes=[pltpu.SemaphoreType.DMA((2,))],
        compiler_params=params(),
        name="stage",
    )(weight_in, weight_out)


def plan_rows(slot_count, ways):
    tiles = slot_count // TILE
    shared = [2, 2] if ways == 2 and tiles >= 8 and tiles % 2 == 0 else []
    alone = (tiles - sum(shared)) // ways
    chunks = [alone - alone // 2, alone // 2]
    return [size * TILE for size in chunks if size], [size * TILE for size in shared]


def starts_of(sizes):
    return [sum(sizes[:k]) for k in range(len(sizes))]


def edge_kernel(ways, place, mine, late, sender_ref, slot_ref, *refs):
    refs = list(refs)

    def take(count):
        taken = refs[:count]
        del refs[:count]
        return taken

    (own, own_gain), mains, others = take(2), take(ways - 1), take(ways - 1 if late else 0)
    nodes, halos = take(ways), take(2 * RADIUS)
    w_in, w_out = take(2)
    others_a, others_b = take(ways - 1), take(ways - 1)
    outs = refs
    width = own.shape[1]
    channels = ways * width
    me = lax.axis_index("chan")
    split, base, start = place
    first = pl.multiple_of(me * split + base, TILE)
    edges = [own[pl.ds(first, mine), :]]
    for d, block in enumerate(mains):
        here = mine - others[d].shape[0] if late else mine
        rows = block[start : start + here, :]
        edges.append(jnp.concatenate([rows, others[d][...]], axis=0) if late else rows)
    local_nodes = nodes[0].shape[0]
    halo_count = sum(h.shape[0] for h in halos)
    to_sender = onehot(column(sender_ref[:, pl.ds(first, mine)]), local_nodes)
    slots = column(slot_ref[:, pl.ds(first, mine)])
    to_slot = onehot(slots, local_nodes + halo_count)
    table = jnp.concatenate([h[...] for h in halos], axis=0)
    preact = None
    for d in range(ways):
        if d == 0:
            weights = (w_in[0], w_in[1], w_in[2])
        else:
            weights = (others_a[d - 1][0], others_a[d - 1][1], others_b[d - 1][0])
        sent = dot(to_sender, nodes[d][...]).astype(bf16)
        got = dot(to_slot[:, :local_nodes], nodes[d][...])
        got = (got + dot(to_slot[:, local_nodes:], table[:, d * width : (d + 1) * width])).astype(bf16)
        term = dot(edges[d], weights[0]) + dot(sent, weights[1]) + dot(got, weights[2])
        preact = term if preact is None else preact + term
    hidden = (0.5 * preact * (1.0 + jnp.tanh(0.5 * preact))).astype(bf16)
    projected = [dot(hidden, w_out[...])]
    for d in range(1, ways):
        blocks = [slice(h * width, (h + 1) * width) for h in range(ways)]
        projected.append(sum(dot(hidden[:, b], others_b[d - 1][1, :, b]) for b in blocks))
    mean = sum(jnp.sum(p, axis=1, keepdims=True) for p in projected) / channels
    square = sum(jnp.sum(p * p, axis=1, keepdims=True) for p in projected) / channels
    scale = lax.rsqrt(square - mean * mean + 1e-05)
    live = jnp.concatenate([slots] * (width // 128), axis=1) >= 0
    for d in range(len(outs)):
        if d == 0:
            gain = own_gain[...]
        else:
            terms = mains[d - 1][mains[d - 1].shape[0] - GAIN_ROWS :, :].astype(f32)
            gain = terms[0:1, :] + terms[1:2, :] + terms[2:3, :]
        normed = (projected[d] - mean) * scale * gain
        outs[d][...] = jnp.where(live, (edges[d].astype(f32) + normed).astype(bf16), edges[d])


def edge_update(k, place, mine, results, senders, slots, own, gain, blocks, others, nodes, halos, w_in, w_out, others_a, others_b):
    ways = len(nodes)
    width = own.shape[1]
    channels = ways * width
    operands = [own, gain, *blocks, *others, *nodes, *halos, w_in, w_out, *others_a, *others_b]
    return pl.pallas_call(
        functools.partial(edge_kernel, ways, place, mine, bool(others)),
        out_shape=[shape(mine, width)] * results,
        in_specs=[VMEM] * (2 + len(operands)),
        out_specs=[VMEM] * results,
        compiler_params=params(),
        cost_estimate=pl.CostEstimate(
            flops=2 * mine * channels * (4 * channels + 768),
            bytes_accessed=8 * channels * channels,
            transcendentals=mine * channels,
        ),
        name=f"edge_update_{k}",
    )(senders, slots, *operands)


def collect_kernel(ways, places, local_nodes, last, slot_ref, *refs):
    refs = list(refs)
    parts = [refs.pop(0) for _ in places]
    sums = refs.pop(0)[...] if len(refs) > (1 + 2 * RADIUS if last else 1) else None
    me = lax.axis_index("chan")
    table_rows = refs[0].shape[0] + (sum(r.shape[0] for r in refs[1:]) if last else 0)
    for (d, split, base), block in zip(places, parts):
        mine = block.shape[0]
        first = pl.multiple_of(lax.rem(me + d, ways) * split + base, TILE)
        slots = slot_ref[:, pl.ds(first, mine)]
        rows = lax.broadcasted_iota(i32, (table_rows, mine), 0)
        hits = (rows == jnp.broadcast_to(slots, (table_rows, mine))).astype(f32).astype(bf16)
        term = dot(hits, block[...])
        sums = term if sums is None else sums + term
    if not last:
        refs[0][...] = sums
        return
    refs[0][...] = sums[:local_nodes]
    start = local_nodes
    for out in refs[1:]:
        size = out.shape[0]
        out[...] = sums[start : start + size].astype(bf16)
        start += size


def collect(places, parts, sums, slots, ways, local_nodes, halo_size, last):
    width = parts[0].shape[1]
    table_rows = local_nodes + 2 * RADIUS * halo_size
    before = [] if sums is None else [sums]
    if last:
        outs = [shape(local_nodes, width, dtype=f32)] + [shape(halo_size, width)] * (2 * RADIUS)
    else:
        outs = [shape(table_rows, width, dtype=f32)]
    return pl.pallas_call(
        functools.partial(collect_kernel, ways, places, local_nodes, last),
        out_shape=outs,
        in_specs=[VMEM] * (1 + len(parts) + len(before)),
        out_specs=[VMEM] * len(outs),
        compiler_params=params(),
        name="collect",
    )(slots, *parts, *before)


def write_kernel(ways, places, *refs):
    parts, out = refs[:-1], refs[-1]
    me = lax.axis_index("chan")
    for (d, split, base), block in zip(places, parts):
        first = pl.multiple_of(lax.rem(me + d, ways) * split + base, TILE)
        out[pl.ds(first, block.shape[0]), :] = block[...]


def write(places, parts, slot_count, ways):
    return pl.pallas_call(
        functools.partial(write_kernel, ways, places),
        out_shape=shape(slot_count, parts[0].shape[1]),
        compiler_params=params(),
        name="write",
    )(*parts)


def finish_kernel(rows_ref, own, *refs):
    returned, out = refs[:-1], refs[-1]
    hits = []
    for j, rows in enumerate(returned):
        ids = lax.broadcasted_iota(i32, (own.shape[0], rows.shape[0]), 0)
        hits.append((ids == jnp.broadcast_to(rows_ref[0, j : j + 1, :], ids.shape)).astype(f32).astype(bf16))
    rows = jnp.concatenate([r[...] for r in returned], axis=0)
    out[...] = own[...] + dot(jnp.concatenate(hits, axis=1), rows)


def finish(halo_rows, own, returned):
    return pl.pallas_call(
        finish_kernel,
        out_shape=shape(*own.shape, dtype=f32),
        compiler_params=params(),
        name="finish",
    )(halo_rows, own, *returned)


def local(
    node_feats,
    edge_feats,
    senders,
    receiver_slot,
    halo_rows,
    tile_counts,
    weight_in,
    weight_out,
    norm_gain,
):
    ways = lax.axis_size("chan")
    offsets = [shift_by for shift_by in range(-RADIUS, RADIUS + 1) if shift_by != 0]
    local_nodes, width = node_feats.shape
    halo_size = halo_rows.shape[2]
    slot_count = edge_feats.shape[0]
    alone, shared = plan_rows(slot_count, ways)
    split, early, late = sum(alone), sum(shared[:1]), sum(shared[1:])
    distances = range(1, ways)
    axes_a, axes_b = even(SHARERS_A), even(SHARERS_B)

    gain = norm_gain.reshape(1, width)
    sender_row, slot_row = senders.reshape(1, -1), mask_slots(tile_counts, receiver_slot.reshape(1, -1))
    message_a = prepare_first(weight_in, axes_a)
    message_b = prepare_second(weight_in, weight_out, ways, axes_b)
    blocks = prepare_blocks(edge_feats, gain, ways, split, early, late)
    blocks = [tie(block, sender_row, slot_row) for block in blocks]
    nodes = [node_feats] + [shifted(node_feats, "chan", d) for d in distances]
    crossed_a = [shifted(message_a, "chan", d) for d in distances]
    crossed_b = [shifted(message_b, "chan", d) for d in distances]
    outgoing = halo_gather(halo_rows, nodes)
    halos = [shifted(rows, ("dom", "rep"), by) for rows, by in zip(outgoing, offsets)]
    edges = [shifted(blocks[d - 1], "chan", d) for d in distances]
    late_edges = [shifted(blocks[-1], "chan", d) for d in distances if late]
    pieces = [tie(piece, *halos[:3]) for piece in crossed_a]
    pieces = [join(piece, swapped(piece, axes_a[0])) for piece in pieces]
    pieces = [tie(piece, *halos[3:]) for piece in pieces]
    crossed_b = [tie(piece, *pieces) for piece in crossed_b]
    groups_a = [(gather_shares(piece, axes_a[1:], []), axes_a) for piece in pieces]
    inner, outer = stage(tie(weight_in, *outgoing), weight_out)
    groups_b = [(gather_shares(piece, axes_b, [inner, outer, *edges]), axes_b) for piece in crossed_b]
    others = assemble(groups_a + groups_b)
    edges = [tie(e, *others) for e in edges]
    others_a, others_b = others[: len(groups_a)], others[len(groups_a) :]

    def collected(places, parts, sums, last=False):
        return collect(places, parts, sums, slot_row, ways, local_nodes, halo_size, last)

    jobs = [(split, before, before, mine, ways) for before, mine in zip(starts_of(alone), alone)]
    if shared:
        jobs.append((0, ways * split, split, early + late, 1))
    parts, places, order = [], [], edge_feats
    for k, (stride, base, start, mine, results) in enumerate(jobs):
        late_rows = late_edges if k == len(alone) else []
        outs = edge_update(
            k, (stride, base, start), mine, results, sender_row, slot_row, order, gain, edges, late_rows,
            nodes, halos, inner, outer, others_a, others_b,
        )
        order = tie(order, *outs)
        outs = [outs[0]] + [shifted(outs[d], "chan", -d) for d in range(1, results)]
        parts.append(outs)
        places.append([(d, stride, base) for d in range(results)])

    def chosen(which):
        return [places[k][d] for k, d in which], [parts[k][d] for k, d in which]

    count = len(alone)
    final = [(count - 1, d) for d in distances]
    own_parts = [(k, 0) for k in range(len(jobs))]
    (sums,) = collected(*chosen(own_parts + [(k, d) for k in range(count - 1) for d in distances]), None)
    own, *pieces = collected(*chosen(final), sums, True)
    returned = [shifted(piece, ("dom", "rep"), -by) for piece, by in zip(pieces, offsets)]
    everything = chosen([(k, d) for k, outs in enumerate(parts) for d in range(len(outs))])
    return (write(*everything, slot_count, ways), finish(halo_rows, own, returned))


def solution(mesh):
    placed = (
        P(("groups", "dom", "rep"), "chan"),
        P(("groups", "dom", "rep"), "chan"),
        P(("groups", "dom", "rep")),
        P(("groups", "dom", "rep")),
        P(("groups", "dom", "rep"), None, None),
        P("groups"),
        P(None, "chan", None),
        P(None, "chan"),
        P("chan"),
    )
    return jax.shard_map(
        local,
        mesh=mesh,
        in_specs=placed,
        out_specs=(P(("groups", "dom", "rep"), "chan"), P(("groups", "dom", "rep"), "chan")),
        check_vma=False,
    )
```
